32 devices in a mesh: tile: 8 (over y, x, core), batch: 4 (over z).
Axes of the slice: x: 2, y: 2, z: 4, core: 2. Of those that a mesh axis runs over, the one named last changes fastest.
Arguments:
- object_tiles: float32 [8, 2, 384, 384], P('tile'), may hold values from -5 to 5
- probe: bfloat16 [8, 2, 256, 256], replicated, may hold values from -4 to 4
- offsets: int32 [8, 4, 2], P('tile', 'batch'), may hold values from 0 to 383, as said below
- amplitude: float32 [8, 4, 256, 256], P('tile', 'batch'), may hold values from 0.3 to 3
Outputs:
- object_grad: float32 [8, 2, 384, 384], P('tile')
- probe_grad: float32 [8, 2, 256, 256], replicated
The draws below stay inside these ranges and needn't reach their ends.
Inputs may be any that keep to these rules, and one draw needn't show every extreme that they name: `offsets`: offsets are such that every patch lies inside the region: in tiles of the last tile row the row offset is at most 128, in tiles of the last tile column the column offset likewise.
All inputs are finite; a program needn't handle non-finite values.
Results may differ from the reference program's by a relative error of at most 0.0003.
Values sent between devices are 32-bit elements; how exact they have to be, the bound alone decides.
A program may use at most 64 MiB of HBM per device.

```python
import math
import jax
import jax.numpy as jnp
from jax import lax

MODES = 8
P_SIZE = 256
TS = 384
TILE_COLS = 4
TILES = 8
POS_TILE = 4
POSITIONS = 32


def draw_offsets(key, part):
    key = jax.random.fold_in(key, 11)
    tile_ids = jnp.arange(TILES, dtype=jnp.int32)
    last_row = tile_ids // TILE_COLS == TILES // TILE_COLS - 1
    last_col = tile_ids % TILE_COLS == TILE_COLS - 1
    limit_y = jnp.where(last_row, TS - P_SIZE + 1, TS)
    limit_x = jnp.where(last_col, TS - P_SIZE + 1, TS)
    limits = jnp.stack([limit_y, limit_x], axis=-1)[:, None, :]
    limits = jnp.broadcast_to(limits, (TILES, POS_TILE, 2)).astype(jnp.int32)
    drawn = jax.random.randint(key, (TILES, POS_TILE, 2), 0, limits, dtype=jnp.int32)
    drawn = drawn.at[0, 0, :].set(TS - 1)
    drawn = drawn.at[0, 1, :].set(0)
    return drawn.astype(jnp.int32)


def block_levels(stream_key, shape, pieces, smallest, top_value):
    factor_of, own = 1.0, jax.random.fold_in(stream_key, 6)
    for axis_at, blocks in pieces:
        draws = jnp.exp(jax.random.uniform(jax.random.fold_in(own, axis_at), (blocks,), jnp.float32, smallest / len(pieces), top_value / len(pieces)))
        factor_of = factor_of * jnp.repeat(draws, shape[axis_at] // blocks).reshape([-1 if axis == axis_at else 1 for axis in range(len(shape))])
    return factor_of


def bell_draw(rng, shape, scale, limit, pieces=(), held_as=jnp.bfloat16):
    values = scale * jax.random.normal(rng, shape, jnp.float32)
    if pieces:
        values = values * block_levels(rng, shape, pieces, -0.22, 0.18)
    return jnp.clip(values, -limit, limit).astype(held_as)


def setup_inputs(seed: int = 0) -> dict:
    streams_of = jax.random.split(jax.random.key(seed), 5)
    return {
        "object_tiles": bell_draw(streams_of[0], (TILES, 2, TS, TS), 0.7, 5.0, ((0, 8),), jnp.float32),
        "probe": bell_draw(streams_of[1], (MODES, 2, P_SIZE, P_SIZE), 0.5, 4.0),
        "offsets": draw_offsets(jax.random.fold_in(streams_of[4], 71), 0),
        "amplitude": jnp.clip(jnp.exp(math.log(3.0) - 2.3025851 * jax.random.uniform(streams_of[3], (TILES, POS_TILE, P_SIZE, P_SIZE), jnp.float32) ** block_levels(streams_of[3], (TILES, POS_TILE, P_SIZE, P_SIZE), ((0, 8), (1, 4)), -0.2, 0.2)), 0.3, 3.0),
    }


def reference(object_tiles, probe, offsets, amplitude):
    tile_rows = TILES // TILE_COLS
    region = object_tiles.reshape(tile_rows, TILE_COLS, 2, TS, TS).transpose(2, 0, 3, 1, 4)
    region = region.reshape(2, tile_rows * TS, TILE_COLS * TS)
    region = jnp.pad(region, ((0, 0), (0, P_SIZE), (0, P_SIZE)))
    tile_ids = jnp.arange(TILES, dtype=jnp.int32)
    base_y = tile_ids // TILE_COLS * TS
    base_x = tile_ids % TILE_COLS * TS
    glob_y = (base_y[:, None] + offsets[:, :, 0]).reshape(-1).astype(jnp.int32)
    glob_x = (base_x[:, None] + offsets[:, :, 1]).reshape(-1).astype(jnp.int32)
    measured = amplitude.reshape(-1, P_SIZE, P_SIZE)
    probe_wide = probe.astype(jnp.float32)
    probe_cplx = probe_wide[:, 0] + 1j * probe_wide[:, 1]
    zero_index = jnp.int32(0)

    def advance(totals, sample):
        grad_region, grad_probe = totals
        row_at, col_at, target = sample
        object_patch = lax.dynamic_slice(region, (zero_index, row_at, col_at), (2, P_SIZE, P_SIZE))
        patch_cplx = object_patch[0] + 1j * object_patch[1]
        far_field = jnp.fft.fft2(probe_cplx * patch_cplx[None], norm='ortho')
        intensity = lax.optimization_barrier(jnp.sum(jnp.real(far_field) ** 2 + jnp.imag(far_field) ** 2, axis=0))
        corrected = far_field * (1.0 - target / jnp.sqrt(intensity + 0.01))[None]
        back_wave = jnp.fft.ifft2(corrected, norm='ortho')
        object_term = lax.optimization_barrier(jnp.sum(jnp.conj(probe_cplx) * back_wave, axis=0))
        old_values = lax.dynamic_slice(grad_region, (zero_index, row_at, col_at), (2, P_SIZE, P_SIZE))
        new_values = old_values + jnp.stack([jnp.real(object_term), jnp.imag(object_term)])
        grad_region = lax.dynamic_update_slice(grad_region, new_values, (zero_index, row_at, col_at))
        grad_probe = grad_probe + jnp.conj(patch_cplx)[None] * back_wave
        return ((grad_region, grad_probe), None)
    start_region = jnp.zeros_like(region)
    start_probe = jnp.zeros_like(probe_cplx)
    (grad_region, grad_probe), _ = lax.scan(advance, (start_region, start_probe), (glob_y, glob_x, measured))
    grad_region = grad_region[:, :tile_rows * TS, :TILE_COLS * TS]
    object_grad = grad_region.reshape(2, tile_rows, TS, TILE_COLS, TS).transpose(1, 3, 0, 2, 4).reshape(TILES, 2, TS, TS)
    probe_grad = jnp.stack([jnp.real(grad_probe), jnp.imag(grad_probe)], axis=1) / jnp.sqrt(jnp.float32(POSITIONS))
    return (object_grad, probe_grad)
```

```python
import functools
import math

import jax
import jax.numpy as jnp
import ml_dtypes
import numpy as np
from jax import lax
from jax.experimental import pallas as pl
from jax.experimental.pallas import tpu as pltpu
from jax.sharding import PartitionSpec as P

TILE_COLS = 4
MESH = pl.DeviceIdType.MESH
F32 = jnp.float32
BF16 = jnp.bfloat16


def split_table(table, axis):
    high = table.astype(np.float32).astype(ml_dtypes.bfloat16)
    low = (table - high.astype(np.float64)).astype(np.float32).astype(ml_dtypes.bfloat16)
    return np.concatenate([high, high, low], axis=axis)


def dft_tables(pattern):
    h = pattern // 2
    n, k = np.arange(h)[:, None], np.arange(h)[None, :]
    even = np.exp(-2j * np.pi * ((2 * n * k) % pattern) / pattern) / math.sqrt(pattern)
    odd = np.exp(-2j * np.pi * ((n * (2 * k + 1)) % pattern) / pattern) / math.sqrt(pattern)

    def right(m):
        return split_table(np.block([[m.real, m.imag], [-m.imag, m.real]]), 0)

    def left(m):
        return split_table(np.block([[m.real, -m.imag], [m.imag, m.real]]), 1)

    rights = np.stack([right(even), right(odd), right(even.conj().T), right(odd.conj().T)])
    lefts = np.stack([left(even.T), left(odd.T), left(even.conj()), left(odd.conj())])
    return rights, lefts


def split(x):
    high = x.astype(BF16)
    return high, (x - high.astype(F32)).astype(BF16)


def times_table(x, table):
    high, low = split(x)
    return jnp.dot(jnp.concatenate([high, low, high], 1), table, preferred_element_type=F32)


def table_times(table, x):
    high, low = split(x)
    return jnp.dot(table, jnp.concatenate([high, low, high], 0), preferred_element_type=F32)


def times_onehot(x, onehot):
    high, low = split(x)
    return jnp.dot(high, onehot, preferred_element_type=F32) + jnp.dot(
        low, onehot, preferred_element_type=F32
    )


def onehot_times(onehot, x):
    high, low = split(x)
    return jnp.dot(onehot, high, preferred_element_type=F32) + jnp.dot(
        onehot, low, preferred_element_type=F32
    )


def onehot(hit):
    return jnp.where(hit, 1.0, 0.0).astype(F32).astype(BF16)


def kernel(n_tile, n_batch, tile_ref, off_ref, amp_ref, probe_ref, right_ref, left_ref,
           og_ref, pg_ref, ext, patch, far, fac, ot, gext, acc, sendbuf, pairbuf, rsbuf, zbuf,
           objbuf, offbuf, xbuf, ybuf, send_sem, recv_sem):
    me = lax.axis_index("tile")
    z = lax.axis_index("batch")
    ts = tile_ref.shape[-1]
    modes, _, ps, _ = probe_ref.shape
    h = ps // 2
    mh = modes // 2
    bits = []
    b = 2
    while b < n_tile:
        bits.append(b)
        b *= 2
    core = lax.rem(me, 2)
    sibling = me + 1 - 2 * core
    col = lax.rem(me, TILE_COLS)
    has_left = col > 0
    has_right = col < TILE_COLS - 1
    has_up = me >= TILE_COLS
    has_down = me < n_tile - TILE_COLS
    count = [0]

    def sems(n=1):
        first = count[0]
        count[0] += n
        return first

    def remote(src, dst, sem, tile, batch):
        return pltpu.make_async_remote_copy(
            src_ref=src, dst_ref=dst, send_sem=send_sem.at[sem], recv_sem=recv_sem.at[sem],
            device_id=(tile, batch), device_id_type=MESH)

    barrier = pltpu.get_barrier_semaphore()

    def greet(tile, batch):
        pl.semaphore_signal(barrier, inc=1, device_id=(tile, batch), device_id_type=MESH)

    greet(sibling, z)
    for b in bits:
        greet(me + b * (1 - 2 * lax.rem(me // b, 2)), z)
    for d in range(1, n_batch):
        greet(me, lax.rem(z + d, n_batch))
    for there, step in ((has_left, -1), (has_right, 1), (has_up, -TILE_COLS), (has_down, TILE_COLS)):
        @pl.when(there)
        def _():
            greet(me + step, z)
    around = sum(jnp.where(t, 1, 0) for t in (has_left, has_right, has_up, has_down))
    pl.semaphore_wait(barrier, 1 + len(bits) + n_batch - 1 + around)

    up = [
        remote(tile_ref.at[:, :ps, :ps], ext.at[:, ts:, :ps], sems(), me - TILE_COLS, z),
        remote(tile_ref.at[:, :ps, ps:], ext.at[:, ts:, ps:ts], sems(), me - TILE_COLS, z),
    ]
    leftward = remote(tile_ref.at[:, :, :ps], ext.at[:, :ts, ts:], sems(), me - 1, z)
    corner = remote(ext.at[:, ts:, :ps], ext.at[:, ts:, ts:], sems(), me - 1, z)

    @pl.when(has_up)
    def _():
        up[0].start()
        up[1].start()

    @pl.when(has_left)
    def _():
        leftward.start()

    ext[:, :ts, :ts] = tile_ref[...]

    @pl.when(jnp.logical_not(has_right))
    def _():
        ext[:, :, ts:] = jnp.zeros((2, ts + ps, ps), F32)

    @pl.when(jnp.logical_not(has_down))
    def _():
        ext[:, ts:, :ts] = jnp.zeros((2, ps, ts), F32)

    @pl.when(jnp.logical_and(jnp.logical_not(has_down), has_right))
    def _():
        ext[:, ts:, ts:] = jnp.zeros((2, ps, ps), F32)

    rows = lax.broadcasted_iota(jnp.int32, (ps, ps), 0)
    cols = lax.broadcasted_iota(jnp.int32, (ps, ps), 1)
    by_row = onehot(cols == jnp.where(rows < h, 2 * rows, 2 * (rows - h) + 1))
    by_col = onehot(rows == jnp.where(cols < h, 2 * cols, 2 * (cols - h) + 1))
    fac[...] = times_onehot(onehot_times(by_row, amp_ref[...]), by_col)

    @pl.when(has_down)
    def _():
        up[0].wait_recv()

    @pl.when(jnp.logical_and(has_down, has_left))
    def _():
        corner.start()

    @pl.when(has_down)
    def _():
        up[1].wait_recv()

    @pl.when(has_right)
    def _():
        leftward.wait_recv()

    @pl.when(jnp.logical_and(has_down, has_right))
    def _():
        corner.wait_recv()

    r_at = off_ref[0:1, 0:1]
    c_at = off_ref[1:2, 0:1]
    te = ts + ps
    pick_r = onehot(lax.broadcasted_iota(jnp.int32, (ps, te), 1)
                    == lax.broadcasted_iota(jnp.int32, (ps, te), 0) + r_at)
    pick_c = onehot(lax.broadcasted_iota(jnp.int32, (te, ps), 0)
                    == lax.broadcasted_iota(jnp.int32, (te, ps), 1) + c_at)
    for part in range(2):
        patch[part] = times_onehot(onehot_times(pick_r, ext[part]), pick_c)

    @pl.when(has_up)
    def _():
        up[0].wait_send()
        up[1].wait_send()

    @pl.when(has_left)
    def _():
        leftward.wait_send()

    @pl.when(jnp.logical_and(has_down, has_left))
    def _():
        corner.wait_send()

    def forward(k, intensity):
        i0, i1 = intensity
        pr, pi = probe_ref[k, 0].astype(F32), probe_ref[k, 1].astype(F32)
        a, b = patch[0], patch[1]
        xr, xi = pr * a - pi * b, pr * b + pi * a
        plus = jnp.concatenate([xr[:, :h] + xr[:, h:], xi[:, :h] + xi[:, h:]], 1)
        minus = jnp.concatenate([xr[:, :h] - xr[:, h:], xi[:, :h] - xi[:, h:]], 1)
        e = times_table(plus, right_ref[0])
        o = times_table(minus, right_ref[1])
        re = jnp.concatenate([e[:, :h], o[:, :h]], 1)
        im = jnp.concatenate([e[:, h:], o[:, h:]], 1)
        g = table_times(left_ref[0], jnp.concatenate([re[:h] + re[h:], im[:h] + im[h:]], 0))
        f = table_times(left_ref[1], jnp.concatenate([re[:h] - re[h:], im[:h] - im[h:]], 0))
        far[k, 0] = g
        far[k, 1] = f
        return (i0 + g[:h] * g[:h] + g[h:] * g[h:], i1 + f[:h] * f[:h] + f[h:] * f[h:])

    zero = jnp.zeros((h, ps), F32)
    i0, i1 = lax.fori_loop(0, modes, forward, (zero, zero))
    fac[:h] = 1.0 - fac[:h] / jnp.sqrt(i0 + 0.01)
    fac[h:] = 1.0 - fac[h:] / jnp.sqrt(i1 + 0.01)
    ot[...] = jnp.zeros_like(ot)

    def backward(k):
        f0, f1 = fac[:h], fac[h:]
        g = far[k, 0] * jnp.concatenate([f0, f0], 0)
        f = far[k, 1] * jnp.concatenate([f1, f1], 0)
        p = table_times(left_ref[2], g)
        q = table_times(left_ref[3], f)
        top, low = p + q, p - q
        re = jnp.concatenate([top[:h], low[:h]], 0)
        im = jnp.concatenate([top[h:], low[h:]], 0)
        e = times_table(jnp.concatenate([re[:, :h], im[:, :h]], 1), right_ref[2])
        o = times_table(jnp.concatenate([re[:, h:], im[:, h:]], 1), right_ref[3])
        br = jnp.concatenate([e[:, :h] + o[:, :h], e[:, :h] - o[:, :h]], 1)
        bi = jnp.concatenate([e[:, h:] + o[:, h:], e[:, h:] - o[:, h:]], 1)
        pr, pi = probe_ref[k, 0].astype(F32), probe_ref[k, 1].astype(F32)
        ot[0] += pr * br + pi * bi
        ot[1] += pr * bi - pi * br
        a, b = patch[0], patch[1]
        return a * br + b * bi, a * bi - b * br

    mode_rows = 2 * ps
    pair = sems(mh)

    def pair_copy(i):
        at = pl.ds(pl.multiple_of(i * mode_rows, mode_rows), mode_rows)
        return remote(sendbuf.at[at], pairbuf.at[at], pair + i, sibling, z)

    def for_sibling(i, carry):
        gr, gi = backward((1 - core) * mh + i)
        at = pl.multiple_of(i * mode_rows, mode_rows)
        sendbuf[pl.ds(at, ps)] = gr
        sendbuf[pl.ds(at + ps, ps)] = gi
        pair_copy(i).start()
        return carry

    lax.fori_loop(0, mh, for_sibling, 0)

    def for_self(i, carry):
        gr, gi = backward(core * mh + i)
        pair_copy(i).wait_recv()
        at = pl.multiple_of(i * mode_rows, mode_rows)
        acc[pl.ds(at, ps)] = gr + pairbuf[pl.ds(at, ps)]
        acc[pl.ds(at + ps, ps)] = gi + pairbuf[pl.ds(at + ps, ps)]
        return carry

    length = mh * mode_rows // 2
    base_out = core * (mh * mode_rows)

    class Stream:
        def __init__(self, index, order):
            self.index, self.order = index, order
            self.first = index * length
            self.start, self.size, self.step = self.first, length, 0
            self.slot = 0
            self.sem_rs = sems(len(order))
            self.sem_ag = sems(len(order))
            self.sem_z = sems(n_batch)
            self.sem_zg = sems(n_batch)
            self.sem_pair = sems()
            self.trail = []

        def rows(self, at, n):
            return pl.ds(pl.multiple_of(at, n), n)

        def rs_start(self):
            b = self.order[self.step]
            mine = lax.rem(me // b, 2)
            half = self.size // 2
            self.partner = me + b * (1 - 2 * mine)
            self.trail.append((self.start, self.size, self.partner, mine))
            self.copy = remote(
                acc.at[self.rows(self.start + (1 - mine) * half, half)],
                rsbuf.at[self.index, pl.ds(self.slot, half)],
                self.sem_rs + self.step, self.partner, z)
            self.copy.start()
            self.start = self.start + mine * half
            self.size = half

        def rs_wait(self):
            self.copy.wait()
            at = self.rows(self.start, self.size)
            acc[at] += rsbuf[self.index, self.slot:self.slot + self.size]
            self.slot += self.size
            self.step += 1

        def z_start(self):
            q = self.size // n_batch
            self.q = q
            self.copies = []
            for d in range(1, n_batch):
                dest = lax.rem(z + d, n_batch)
                c = remote(acc.at[self.rows(self.start + dest * q, q)], zbuf.at[self.index, d],
                           self.sem_z + d, me, dest)
                c.start()
                self.copies.append(c)

        def z_wait(self):
            for c in self.copies:
                c.wait()
            total = acc[self.rows(self.start + z * self.q, self.q)]
            for d in range(1, n_batch):
                total = total + zbuf[self.index, d]
            at = self.rows(base_out + self.start + z * self.q, self.q)
            pg_ref[at] = total
            self.copies = []
            for d in range(1, n_batch):
                c = remote(pg_ref.at[at], pg_ref.at[at], self.sem_zg + d, me, lax.rem(z + d, n_batch))
                c.start()
                self.copies.append(c)

        def zg_wait(self):
            for c in self.copies:
                c.wait()

        def ag_start(self):
            self.step -= 1
            start, size, partner, mine = self.trail[self.step]
            at = self.rows(base_out + start + mine * (size // 2), size // 2)
            self.copy = remote(pg_ref.at[at], pg_ref.at[at], self.sem_ag + self.step, partner, z)
            self.copy.start()

        def ag_wait(self):
            self.copy.wait()

        def pair_start(self):
            at = self.rows(base_out + self.first, length)
            self.copy = remote(pg_ref.at[at], pg_ref.at[at], self.sem_pair, sibling, z)
            self.copy.start()

    streams = [Stream(0, bits), Stream(1, bits[::-1])]

    lax.fori_loop(0, mh // 2, for_self, 0)
    streams[0].rs_start()
    lax.fori_loop(mh // 2, mh, for_self, 0)
    streams[1].rs_start()

    osem, fsem = sems(n_batch), sems(n_batch)
    objects = []
    for d in range(1, n_batch):
        dest = lax.rem(z + d, n_batch)
        objects.append(remote(off_ref, offbuf.at[d], fsem + d, me, dest))
        objects.append(remote(ot, objbuf.at[d], osem + d, me, dest))
    for c in objects:
        c.start()

    for step in range(len(bits)):
        for s in streams:
            s.rs_wait()
            if step + 1 < len(bits):
                s.rs_start()
            else:
                s.z_start()

    for c in objects:
        c.wait()
    right_sem, down_sem = sems(2), sems(2)
    rightward, downward = [], []
    for part in range(2):
        total = None
        for d in range(n_batch):
            offs = off_ref if d == 0 else offbuf.at[d]
            term = ot[part] if d == 0 else objbuf[d, part]
            put_r = onehot(lax.broadcasted_iota(jnp.int32, (te, ps), 0)
                           == lax.broadcasted_iota(jnp.int32, (te, ps), 1) + offs[0:1, 0:1])
            put_c = onehot(lax.broadcasted_iota(jnp.int32, (ps, te), 1)
                           == lax.broadcasted_iota(jnp.int32, (ps, te), 0) + offs[1:2, 0:1])
            if d == 0:
                gext[part] = times_onehot(onehot_times(put_r, term), put_c)
            else:
                gext[part] += times_onehot(onehot_times(put_r, term), put_c)
        c = remote(gext.at[part, :, ts:], xbuf.at[part], right_sem + part, me + 1, z)
        rightward.append(c)

        @pl.when(has_right)
        def _():
            c.start()

    for s in streams:
        s.z_wait()

    for part in range(2):
        @pl.when(has_left)
        def _():
            rightward[part].wait_recv()
            gext[part, :, :ps] += xbuf[part]

        c = remote(gext.at[part, ts:, :ts], ybuf.at[part], down_sem + part, me + TILE_COLS, z)
        downward.append(c)

        @pl.when(has_down)
        def _():
            c.start()

    for s in streams:
        s.zg_wait()
        s.ag_start()
    for step in range(len(bits)):
        for s in streams:
            s.ag_wait()
            if step + 1 < len(bits):
                s.ag_start()
            else:
                s.pair_start()

    for part in range(2):
        og_ref[part] = gext[part, :ts, :ts]

        @pl.when(has_up)
        def _():
            downward[part].wait_recv()
            og_ref[part, :ps, :] += ybuf[part]

    for part in range(2):
        @pl.when(has_right)
        def _():
            rightward[part].wait_send()

        @pl.when(has_down)
        def _():
            downward[part].wait_send()

    for s in streams:
        s.copy.wait()

    def sent(i, carry):
        pair_copy(i).wait_send()
        return carry

    lax.fori_loop(0, mh, sent, 0)


def n_sems(n_tile, n_batch, modes):
    n_bits = n_tile.bit_length() - 2
    return 4 + modes // 2 + 2 * (2 * n_bits + 2 * n_batch + 1) + 2 * n_batch + 4


def shards(n_tile, n_batch, object_tiles, probe, offsets, amplitude):
    modes, _, ps, _ = probe.shape
    ts = object_tiles.shape[-1]
    te = ts + ps
    rights, lefts = dft_tables(ps)
    held = jnp.broadcast_to(jnp.pad(offsets[0, 0], (0, 6))[:, None], (8, 128))
    n = n_sems(n_tile, n_batch, modes)
    half = modes // 2 * 2 * ps
    quarter = half // 2
    q = quarter // (n_tile // 2) // n_batch
    vmem = pl.BlockSpec(memory_space=pltpu.VMEM)
    og, pg = pl.pallas_call(
        functools.partial(kernel, n_tile, n_batch),
        out_shape=(jax.ShapeDtypeStruct((2, ts, ts), F32),
                   jax.ShapeDtypeStruct((modes * 2 * ps, ps), F32)),
        in_specs=[vmem] * 6,
        out_specs=(vmem, vmem),
        scratch_shapes=[
            pltpu.VMEM((2, te, te), F32),
            pltpu.VMEM((2, ps, ps), F32),
            pltpu.VMEM((modes, 2, ps, ps), F32),
            pltpu.VMEM((ps, ps), F32),
            pltpu.VMEM((2, ps, ps), F32),
            pltpu.VMEM((2, te, te), F32),
            pltpu.VMEM((half, ps), F32),
            pltpu.VMEM((half, ps), F32),
            pltpu.VMEM((half, ps), F32),
            pltpu.VMEM((2, quarter, ps), F32),
            pltpu.VMEM((2, n_batch, q, ps), F32),
            pltpu.VMEM((n_batch, 2, ps, ps), F32),
            pltpu.VMEM((n_batch, 8, 128), jnp.int32),
            pltpu.VMEM((2, te, ps), F32),
            pltpu.VMEM((2, ps, ts), F32),
            pltpu.SemaphoreType.DMA((n,)),
            pltpu.SemaphoreType.DMA((n,)),
        ],
        compiler_params=pltpu.CompilerParams(
            collective_id=0, has_side_effects=True, vmem_limit_bytes=56 * 1024 * 1024),
        cost_estimate=pl.CostEstimate(flops=13_000_000_000, bytes_accessed=20_000_000, transcendentals=0),
        name="ptycho",
    )(object_tiles[0], held, amplitude[0, 0], probe, rights, lefts)
    positions = n_tile * n_batch * offsets.shape[1]
    return og[None], pg.reshape(modes, 2, ps, ps) * (1.0 / math.sqrt(positions))


def solution(mesh):
    placed = (
        P("tile", None, None, None),
        P(),
        P("tile", "batch", None),
        P("tile", "batch", None, None),
    )
    return jax.shard_map(
        functools.partial(shards, mesh.shape["tile"], mesh.shape["batch"]),
        mesh=mesh,
        in_specs=placed,
        out_specs=(P("tile", None, None, None), P()),
        check_vma=False,
    )
```

```python
import functools
import math

import jax
import jax.numpy as jnp
import ml_dtypes
import numpy as np
from jax import lax
from jax.experimental import pallas as pl
from jax.experimental.pallas import tpu as pltpu
from jax.sharding import PartitionSpec as P

TILE_COLS = 4
MESH = pl.DeviceIdType.MESH
F32 = jnp.float32
BF16 = jnp.bfloat16


def split_table(table, axis):
    high = table.astype(np.float32).astype(ml_dtypes.bfloat16)
    low = (table - high.astype(np.float64)).astype(np.float32).astype(ml_dtypes.bfloat16)
    return np.concatenate([high, high, low], axis=axis)


def dft_tables(pattern):
    h = pattern // 2
    n, k = np.arange(h)[:, None], np.arange(h)[None, :]
    even = np.exp(-2j * np.pi * ((2 * n * k) % pattern) / pattern) / math.sqrt(pattern)
    odd = np.exp(-2j * np.pi * ((n * (2 * k + 1)) % pattern) / pattern) / math.sqrt(pattern)

    def right(m):
        return split_table(np.block([[m.real, m.imag], [-m.imag, m.real]]), 0)

    def left(m):
        return split_table(np.block([[m.real, -m.imag], [m.imag, m.real]]), 1)

    rights = np.stack([right(even), right(odd), right(even.conj().T), right(odd.conj().T)])
    lefts = np.stack([left(even.T), left(odd.T), left(even.conj()), left(odd.conj())])
    return rights, lefts


def split(x):
    high = x.astype(BF16)
    return high, (x - high.astype(F32)).astype(BF16)


def times_table(x, table):
    high, low = split(x)
    return jnp.dot(jnp.concatenate([high, low, high], 1), table, preferred_element_type=F32)


def table_times(table, x):
    high, low = split(x)
    return jnp.dot(table, jnp.concatenate([high, low, high], 0), preferred_element_type=F32)


def times_onehot(x, onehot):
    high, low = split(x)
    return jnp.dot(high, onehot, preferred_element_type=F32) + jnp.dot(
        low, onehot, preferred_element_type=F32
    )


def onehot_times(onehot, x):
    high, low = split(x)
    return jnp.dot(onehot, high, preferred_element_type=F32) + jnp.dot(
        onehot, low, preferred_element_type=F32
    )


def onehot(hit):
    return jnp.where(hit, 1.0, 0.0).astype(F32).astype(BF16)


def kernel(n_tile, n_batch, tile_ref, off_ref, amp_ref, probe_ref, right_ref, left_ref,
           og_ref, pg_ref, ext, patch, far, fac, ot, gext, acc, sendbuf, pairbuf, rsbuf, zbuf,
           objbuf, offbuf, xbuf, ybuf, send_sem, recv_sem):
    me = lax.axis_index("tile")
    z = lax.axis_index("batch")
    ts = tile_ref.shape[-1]
    modes, _, ps, _ = probe_ref.shape
    h = ps // 2
    mh = modes // 2
    bits = []
    b = 2
    while b < n_tile:
        bits.append(b)
        b *= 2
    core = lax.rem(me, 2)
    sibling = me + 1 - 2 * core
    col = lax.rem(me, TILE_COLS)
    has_left = col > 0
    has_right = col < TILE_COLS - 1
    has_up = me >= TILE_COLS
    has_down = me < n_tile - TILE_COLS
    count = [0]

    def sems(n=1):
        first = count[0]
        count[0] += n
        return first

    def remote(src, dst, sem, tile, batch):
        return pltpu.make_async_remote_copy(
            src_ref=src, dst_ref=dst, send_sem=send_sem.at[sem], recv_sem=recv_sem.at[sem],
            device_id=(tile, batch), device_id_type=MESH)

    barrier = pltpu.get_barrier_semaphore()

    def greet(tile, batch):
        pl.semaphore_signal(barrier, inc=1, device_id=(tile, batch), device_id_type=MESH)

    greet(sibling, z)
    for b in bits:
        greet(me + b * (1 - 2 * lax.rem(me // b, 2)), z)
    for d in range(1, n_batch):
        greet(me, lax.rem(z + d, n_batch))
    for there, step in ((has_left, -1), (has_right, 1), (has_up, -TILE_COLS), (has_down, TILE_COLS)):
        @pl.when(there)
        def _():
            greet(me + step, z)
    around = sum(jnp.where(t, 1, 0) for t in (has_left, has_right, has_up, has_down))
    pl.semaphore_wait(barrier, 1 + len(bits) + n_batch - 1 + around)

    fsem = sems(n_batch)
    offs_out = [remote(off_ref, offbuf.at[d], fsem + d, me, lax.rem(z + d, n_batch))
                for d in range(1, n_batch)]
    for c in offs_out:
        c.start()

    up = [
        remote(tile_ref.at[:, :ps, :ps], ext.at[:, ts:, :ps], sems(), me - TILE_COLS, z),
        remote(tile_ref.at[:, :ps, ps:], ext.at[:, ts:, ps:ts], sems(), me - TILE_COLS, z),
    ]
    leftward = remote(tile_ref.at[:, :, :ps], ext.at[:, :ts, ts:], sems(), me - 1, z)
    corner = remote(ext.at[:, ts:, :ps], ext.at[:, ts:, ts:], sems(), me - 1, z)

    @pl.when(has_up)
    def _():
        up[0].start()
        up[1].start()

    @pl.when(has_left)
    def _():
        leftward.start()

    ext[:, :ts, :ts] = tile_ref[...]

    @pl.when(jnp.logical_not(has_right))
    def _():
        ext[:, :, ts:] = jnp.zeros((2, ts + ps, ps), F32)

    @pl.when(jnp.logical_not(has_down))
    def _():
        ext[:, ts:, :ts] = jnp.zeros((2, ps, ts), F32)

    @pl.when(jnp.logical_and(jnp.logical_not(has_down), has_right))
    def _():
        ext[:, ts:, ts:] = jnp.zeros((2, ps, ps), F32)

    rows = lax.broadcasted_iota(jnp.int32, (ps, ps), 0)
    cols = lax.broadcasted_iota(jnp.int32, (ps, ps), 1)
    by_row = onehot(cols == jnp.where(rows < h, 2 * rows, 2 * (rows - h) + 1))
    by_col = onehot(rows == jnp.where(cols < h, 2 * cols, 2 * (cols - h) + 1))
    fac[...] = times_onehot(onehot_times(by_row, amp_ref[...]), by_col)

    @pl.when(has_down)
    def _():
        up[0].wait_recv()

    @pl.when(jnp.logical_and(has_down, has_left))
    def _():
        corner.start()

    @pl.when(has_down)
    def _():
        up[1].wait_recv()

    @pl.when(has_right)
    def _():
        leftward.wait_recv()

    @pl.when(jnp.logical_and(has_down, has_right))
    def _():
        corner.wait_recv()

    r_at = off_ref[0:1, 0:1]
    c_at = off_ref[1:2, 0:1]
    te = ts + ps
    pick_r = onehot(lax.broadcasted_iota(jnp.int32, (ps, te), 1)
                    == lax.broadcasted_iota(jnp.int32, (ps, te), 0) + r_at)
    pick_c = onehot(lax.broadcasted_iota(jnp.int32, (te, ps), 0)
                    == lax.broadcasted_iota(jnp.int32, (te, ps), 1) + c_at)
    for part in range(2):
        patch[part] = times_onehot(onehot_times(pick_r, ext[part]), pick_c)

    @pl.when(has_up)
    def _():
        up[0].wait_send()
        up[1].wait_send()

    @pl.when(has_left)
    def _():
        leftward.wait_send()

    @pl.when(jnp.logical_and(has_down, has_left))
    def _():
        corner.wait_send()

    def forward(k, intensity):
        i0, i1 = intensity
        pr, pi = probe_ref[k, 0].astype(F32), probe_ref[k, 1].astype(F32)
        a, b = patch[0], patch[1]
        xr, xi = pr * a - pi * b, pr * b + pi * a
        plus = jnp.concatenate([xr[:, :h] + xr[:, h:], xi[:, :h] + xi[:, h:]], 1)
        minus = jnp.concatenate([xr[:, :h] - xr[:, h:], xi[:, :h] - xi[:, h:]], 1)
        e = times_table(plus, right_ref[0])
        o = times_table(minus, right_ref[1])
        re = jnp.concatenate([e[:, :h], o[:, :h]], 1)
        im = jnp.concatenate([e[:, h:], o[:, h:]], 1)
        g = table_times(left_ref[0], jnp.concatenate([re[:h] + re[h:], im[:h] + im[h:]], 0))
        f = table_times(left_ref[1], jnp.concatenate([re[:h] - re[h:], im[:h] - im[h:]], 0))
        far[k, 0] = g
        far[k, 1] = f
        return (i0 + g[:h] * g[:h] + g[h:] * g[h:], i1 + f[:h] * f[:h] + f[h:] * f[h:])

    zero = jnp.zeros((h, ps), F32)
    i0, i1 = lax.fori_loop(
        0, modes // 2, lambda i, c: forward(2 * i + 1, forward(2 * i, c)), (zero, zero))
    fac[:h] = 1.0 - fac[:h] / jnp.sqrt(i0 + 0.01)
    fac[h:] = 1.0 - fac[h:] / jnp.sqrt(i1 + 0.01)
    ot[...] = jnp.zeros_like(ot)

    def backward(k):
        f0, f1 = fac[:h], fac[h:]
        g = far[k, 0] * jnp.concatenate([f0, f0], 0)
        f = far[k, 1] * jnp.concatenate([f1, f1], 0)
        p = table_times(left_ref[2], g)
        q = table_times(left_ref[3], f)
        top, low = p + q, p - q
        re = jnp.concatenate([top[:h], low[:h]], 0)
        im = jnp.concatenate([top[h:], low[h:]], 0)
        e = times_table(jnp.concatenate([re[:, :h], im[:, :h]], 1), right_ref[2])
        o = times_table(jnp.concatenate([re[:, h:], im[:, h:]], 1), right_ref[3])
        br = jnp.concatenate([e[:, :h] + o[:, :h], e[:, :h] - o[:, :h]], 1)
        bi = jnp.concatenate([e[:, h:] + o[:, h:], e[:, h:] - o[:, h:]], 1)
        pr, pi = probe_ref[k, 0].astype(F32), probe_ref[k, 1].astype(F32)
        ot[0] += pr * br + pi * bi
        ot[1] += pr * bi - pi * br
        a, b = patch[0], patch[1]
        return a * br + b * bi, a * bi - b * br

    mode_rows = 2 * ps
    pair = sems(mh)

    def pair_copy(i):
        at = pl.ds(pl.multiple_of(i * mode_rows, mode_rows), mode_rows)
        return remote(sendbuf.at[at], pairbuf.at[at], pair + i, sibling, z)

    def both(i):
        gr, gi = backward((1 - core) * mh + i)
        at = pl.multiple_of(i * mode_rows, mode_rows)
        sendbuf[pl.ds(at, ps)] = gr
        sendbuf[pl.ds(at + ps, ps)] = gi
        pair_copy(i).start()
        gr, gi = backward(core * mh + i)
        pair_copy(i).wait_recv()
        acc[pl.ds(at, ps)] = gr + pairbuf[pl.ds(at, ps)]
        acc[pl.ds(at + ps, ps)] = gi + pairbuf[pl.ds(at + ps, ps)]

    n_streams = streams_of(n_tile, n_batch, mh, mode_rows)
    length = mh * mode_rows // n_streams
    per_stream = mh // n_streams
    stream_sems = 2 * len(bits) + 2 * n_batch + 1
    base_out = core * (mh * mode_rows)

    class Stream:
        def __init__(self, index, order):
            self.index, self.order = index, order
            self.first = index * length
            self.start, self.size, self.step = self.first, length, 0
            self.slot = 0
            self.sem_rs = stream_base + index * stream_sems
            self.sem_ag = self.sem_rs + len(order)
            self.sem_z = self.sem_ag + len(order)
            self.sem_zg = self.sem_z + n_batch
            self.sem_pair = self.sem_zg + n_batch
            self.trail = []

        def rows(self, at, n):
            return pl.ds(pl.multiple_of(at, n), n)

        def rs_start(self):
            b = self.order[self.step]
            mine = lax.rem(me // b, 2)
            half = self.size // 2
            self.partner = me + b * (1 - 2 * mine)
            self.trail.append((self.start, self.size, self.partner, mine))
            self.copy = remote(
                acc.at[self.rows(self.start + (1 - mine) * half, half)],
                rsbuf.at[self.index, pl.ds(self.slot, half)],
                self.sem_rs + self.step, self.partner, z)
            if self.step:
                self.copy.start()
            self.start = self.start + mine * half
            self.size = half

        def rs_wait(self):
            self.copy.wait()
            at = self.rows(self.start, self.size)
            acc[at] += rsbuf[self.index, self.slot:self.slot + self.size]
            self.slot += self.size
            self.step += 1

        def z_start(self):
            q = self.size // n_batch
            self.q = q
            self.copies = []
            for d in range(1, n_batch):
                dest = lax.rem(z + d, n_batch)
                c = remote(acc.at[self.rows(self.start + dest * q, q)], zbuf.at[self.index, d],
                           self.sem_z + d, me, dest)
                c.start()
                self.copies.append(c)

        def z_wait(self):
            for c in self.copies:
                c.wait()
            total = acc[self.rows(self.start + z * self.q, self.q)]
            for d in range(1, n_batch):
                total = total + zbuf[self.index, d]
            at = self.rows(base_out + self.start + z * self.q, self.q)
            pg_ref[at] = total
            self.copies = []
            for d in range(1, n_batch):
                c = remote(pg_ref.at[at], pg_ref.at[at], self.sem_zg + d, me, lax.rem(z + d, n_batch))
                c.start()
                self.copies.append(c)

        def zg_wait(self):
            for c in self.copies:
                c.wait()

        def ag_start(self):
            self.step -= 1
            start, size, partner, mine = self.trail[self.step]
            at = self.rows(base_out + start + mine * (size // 2), size // 2)
            self.copy = remote(pg_ref.at[at], pg_ref.at[at], self.sem_ag + self.step, partner, z)
            self.copy.start()

        def ag_wait(self):
            self.copy.wait()

        def pair_start(self):
            at = self.rows(base_out + self.first, length)
            self.copy = remote(pg_ref.at[at], pg_ref.at[at], self.sem_pair, sibling, z)
            self.copy.start()

    stream_base = sems(n_streams * stream_sems)

    def summed(i, carry):
        for j in range(per_stream):
            both(i * per_stream + j)
        bit = bits[0] + lax.rem(i, 2) * (bits[-1] - bits[0])
        mine = lax.rem(me // bit, 2)
        half = length // 2
        at = pl.multiple_of(i * length + (1 - mine) * half, half)
        remote(acc.at[pl.ds(at, half)], rsbuf.at[i, pl.ds(0, half)],
               stream_base + i * stream_sems, me + bit * (1 - 2 * mine), z).start()
        return carry

    lax.fori_loop(0, n_streams, summed, 0)
    streams = [Stream(i, bits if i % 2 == 0 else bits[::-1]) for i in range(n_streams)]
    for s in streams:
        s.rs_start()

    osem = sems(2 * n_batch)

    def passing(way, stage):
        origin = z - way * stage
        sends = jnp.logical_and(
            jnp.logical_and(origin >= 0, origin < n_batch),
            jnp.logical_and(z + way >= 0, z + way < n_batch))
        at = jnp.clip(origin, 0, n_batch - 1)
        src = ot if stage == 0 else objbuf.at[at]
        to = jnp.clip(z + way, 0, n_batch - 1)
        return sends, remote(src, objbuf.at[at], osem + stage + (n_batch if way < 0 else 0), me, to)

    def arrival(way, stage):
        origin = z - way * (1 + stage)
        comes = jnp.logical_and(origin >= 0, origin < n_batch)
        at = jnp.clip(origin, 0, n_batch - 1)
        return comes, at, remote(ot, objbuf.at[at], osem + stage + (n_batch if way < 0 else 0),
                                 me, jnp.clip(z + way, 0, n_batch - 1))

    def start_passing(stage):
        for way in (1, -1):
            sends, c = passing(way, stage)

            @pl.when(sends)
            def _():
                c.start()

    def place(offs, term, part):
        put_r = onehot(lax.broadcasted_iota(jnp.int32, (te, ps), 0)
                       == lax.broadcasted_iota(jnp.int32, (te, ps), 1) + offs[0:1, 0:1])
        put_c = onehot(lax.broadcasted_iota(jnp.int32, (ps, te), 1)
                       == lax.broadcasted_iota(jnp.int32, (ps, te), 0) + offs[1:2, 0:1])
        return onehot_times(put_r, times_onehot(term, put_c))

    def arrived(stage):
        for way in (1, -1):
            comes, at, c = arrival(way, stage)

            @pl.when(comes)
            def _():
                c.wait_recv()
        if stage + 1 < n_batch - 1:
            start_passing(stage + 1)
        for way in (1, -1):
            comes, at, c = arrival(way, stage)
            slot = stage + 1 if way > 0 else n_batch - 1 - stage

            @pl.when(comes)
            def _():
                for part in range(2):
                    gext[part] += place(offbuf.at[slot], objbuf[at, part], part)

    start_passing(0)
    for part in range(2):
        gext[part] = place(off_ref, ot[part], part)
    for c in offs_out:
        c.wait()

    for step in range(len(bits)):
        for s in streams:
            s.rs_wait()
            if step + 1 < len(bits):
                s.rs_start()
            else:
                s.z_start()

    for stage in range(n_batch - 1):
        arrived(stage)
    right_sem, down_sem = sems(2), sems(2)
    rightward, downward = [], []
    for part in range(2):
        c = remote(gext.at[part, :, ts:], xbuf.at[part], right_sem + part, me + 1, z)
        rightward.append(c)

        @pl.when(has_right)
        def _():
            c.start()

    for s in streams:
        s.z_wait()

    for part in range(2):
        @pl.when(has_left)
        def _():
            rightward[part].wait_recv()
            gext[part, :, :ps] += xbuf[part]

        c = remote(gext.at[part, ts:, :ts], ybuf.at[part], down_sem + part, me + TILE_COLS, z)
        downward.append(c)

        @pl.when(has_down)
        def _():
            c.start()

    for s in streams:
        s.zg_wait()
        s.ag_start()
    for step in range(len(bits)):
        for s in streams:
            s.ag_wait()
            if step + 1 < len(bits):
                s.ag_start()
            else:
                s.pair_start()

    for part in range(2):
        og_ref[part] = gext[part, :ts, :ts]

        @pl.when(has_up)
        def _():
            downward[part].wait_recv()
            og_ref[part, :ps, :] += ybuf[part]

    for part in range(2):
        @pl.when(has_right)
        def _():
            rightward[part].wait_send()

        @pl.when(has_down)
        def _():
            downward[part].wait_send()

    for s in streams:
        s.copy.wait()

    for stage in range(n_batch - 1):
        for way in (1, -1):
            sends, c = passing(way, stage)

            @pl.when(sends)
            def _():
                c.wait_send()

    def sent(i, carry):
        pair_copy(i).wait_send()
        return carry

    lax.fori_loop(0, mh, sent, 0)


def streams_of(n_tile, n_batch, mh, mode_rows):
    return mh if mode_rows // (n_tile // 2) // n_batch >= 8 else 2


def n_sems(n_tile, n_batch, mh, n_streams):
    n_bits = n_tile.bit_length() - 2
    return 4 + mh + n_streams * (2 * n_bits + 2 * n_batch + 1) + 3 * n_batch + 4


def shards(n_tile, n_batch, object_tiles, probe, offsets, amplitude):
    modes, _, ps, _ = probe.shape
    ts = object_tiles.shape[-1]
    te = ts + ps
    rights, lefts = dft_tables(ps)
    held = jnp.broadcast_to(jnp.pad(offsets[0, 0], (0, 6))[:, None], (8, 128))
    n_streams = streams_of(n_tile, n_batch, modes // 2, 2 * ps)
    n = n_sems(n_tile, n_batch, modes // 2, n_streams)
    half = modes // 2 * 2 * ps
    length = half // n_streams
    q = length // (n_tile // 2) // n_batch
    vmem = pl.BlockSpec(memory_space=pltpu.VMEM)
    og, pg = pl.pallas_call(
        functools.partial(kernel, n_tile, n_batch),
        out_shape=(jax.ShapeDtypeStruct((2, ts, ts), F32),
                   jax.ShapeDtypeStruct((modes * 2 * ps, ps), F32)),
        in_specs=[vmem] * 6,
        out_specs=(vmem, vmem),
        scratch_shapes=[
            pltpu.VMEM((2, te, te), F32),
            pltpu.VMEM((2, ps, ps), F32),
            pltpu.VMEM((modes, 2, ps, ps), F32),
            pltpu.VMEM((ps, ps), F32),
            pltpu.VMEM((2, ps, ps), F32),
            pltpu.VMEM((2, te, te), F32),
            pltpu.VMEM((half, ps), F32),
            pltpu.VMEM((half, ps), F32),
            pltpu.VMEM((half, ps), F32),
            pltpu.VMEM((n_streams, length, ps), F32),
            pltpu.VMEM((n_streams, n_batch, q, ps), F32),
            pltpu.VMEM((n_batch, 2, ps, ps), F32),
            pltpu.VMEM((n_batch, 8, 128), jnp.int32),
            pltpu.VMEM((2, te, ps), F32),
            pltpu.VMEM((2, ps, ts), F32),
            pltpu.SemaphoreType.DMA((n,)),
            pltpu.SemaphoreType.DMA((n,)),
        ],
        compiler_params=pltpu.CompilerParams(
            collective_id=0, has_side_effects=True, vmem_limit_bytes=56 * 1024 * 1024),
        cost_estimate=pl.CostEstimate(flops=13_000_000_000, bytes_accessed=20_000_000, transcendentals=0),
        name="ptycho",
    )(object_tiles[0], held, amplitude[0, 0], probe, rights, lefts)
    positions = n_tile * n_batch * offsets.shape[1]
    return og[None], pg.reshape(modes, 2, ps, ps) * (1.0 / math.sqrt(positions))


def solution(mesh):
    placed = (
        P("tile", None, None, None),
        P(),
        P("tile", "batch", None),
        P("tile", "batch", None, None),
    )
    return jax.shard_map(
        functools.partial(shards, mesh.shape["tile"], mesh.shape["batch"]),
        mesh=mesh,
        in_specs=placed,
        out_specs=(P("tile", None, None, None), P()),
        check_vma=False,
    )
```

```python
import functools
import math

import jax
import jax.numpy as jnp
import ml_dtypes
import numpy as np
from jax import lax
from jax.experimental import pallas as pl
from jax.experimental.pallas import tpu as pltpu
from jax.sharding import PartitionSpec as P

TILE_COLS = 4
MESH = pl.DeviceIdType.MESH
F32 = jnp.float32
BF16 = jnp.bfloat16


def split_table(table, axis):
    high = table.astype(np.float32).astype(ml_dtypes.bfloat16)
    low = (table - high.astype(np.float64)).astype(np.float32).astype(ml_dtypes.bfloat16)
    return np.concatenate([high, high, low], axis=axis)


def dft_tables(pattern):
    h = pattern // 2
    n, k = np.arange(h)[:, None], np.arange(h)[None, :]
    even = np.exp(-2j * np.pi * ((2 * n * k) % pattern) / pattern) / math.sqrt(pattern)
    odd = np.exp(-2j * np.pi * ((n * (2 * k + 1)) % pattern) / pattern) / math.sqrt(pattern)

    def right(m):
        return split_table(np.block([[m.real, m.imag], [-m.imag, m.real]]), 0)

    def left(m):
        return split_table(np.block([[m.real, -m.imag], [m.imag, m.real]]), 1)

    rights = np.stack([right(even), right(odd), right(even.conj().T), right(odd.conj().T)])
    lefts = np.stack([left(even.T), left(odd.T), left(even.conj()), left(odd.conj())])
    return rights, lefts


def split(x):
    high = x.astype(BF16)
    return high, (x - high.astype(F32)).astype(BF16)


def times_table(x, table):
    high, low = split(x)
    return jnp.dot(jnp.concatenate([high, low, high], 1), table, preferred_element_type=F32)


def table_times(table, x):
    high, low = split(x)
    return jnp.dot(table, jnp.concatenate([high, low, high], 0), preferred_element_type=F32)


def times_onehot(x, onehot):
    high, low = split(x)
    return jnp.dot(high, onehot, preferred_element_type=F32) + jnp.dot(
        low, onehot, preferred_element_type=F32
    )


def onehot_times(onehot, x):
    high, low = split(x)
    return jnp.dot(onehot, high, preferred_element_type=F32) + jnp.dot(
        onehot, low, preferred_element_type=F32
    )


def onehot(hit):
    return jnp.where(hit, 1.0, 0.0).astype(F32).astype(BF16)


def kernel(n_tile, n_batch, tile_ref, off_ref, amp_ref, probe_ref, right_ref, left_ref,
           og_ref, pg_ref, ext, patch, far, fac, ot, gext, acc, sendbuf, pairbuf, rsbuf, zbuf,
           objbuf, offbuf, xbuf, ybuf, send_sem, recv_sem):
    me = lax.axis_index("tile")
    z = lax.axis_index("batch")
    ts = tile_ref.shape[-1]
    modes, _, ps, _ = probe_ref.shape
    h = ps // 2
    mh = modes // 2
    bits = []
    b = 2
    while b < n_tile:
        bits.append(b)
        b *= 2
    core = lax.rem(me, 2)
    sibling = me + 1 - 2 * core
    col = lax.rem(me, TILE_COLS)
    has_left = col > 0
    has_right = col < TILE_COLS - 1
    has_up = me >= TILE_COLS
    has_down = me < n_tile - TILE_COLS
    count = [0]

    def sems(n=1):
        first = count[0]
        count[0] += n
        return first

    def remote(src, dst, sem, tile, batch):
        return pltpu.make_async_remote_copy(
            src_ref=src, dst_ref=dst, send_sem=send_sem.at[sem], recv_sem=recv_sem.at[sem],
            device_id=(tile, batch), device_id_type=MESH)

    barrier = pltpu.get_barrier_semaphore()

    def greet(tile, batch):
        pl.semaphore_signal(barrier, inc=1, device_id=(tile, batch), device_id_type=MESH)

    greet(sibling, z)
    for b in bits:
        greet(me + b * (1 - 2 * lax.rem(me // b, 2)), z)
    for d in range(1, n_batch):
        greet(me, lax.rem(z + d, n_batch))
    for there, step in ((has_left, -1), (has_right, 1), (has_up, -TILE_COLS), (has_down, TILE_COLS)):
        @pl.when(there)
        def _():
            greet(me + step, z)
    around = sum(jnp.where(t, 1, 0) for t in (has_left, has_right, has_up, has_down))
    pl.semaphore_wait(barrier, 1 + len(bits) + n_batch - 1 + around)

    fsem = sems(n_batch)
    offs_out = [remote(off_ref, offbuf.at[d], fsem + d, me, lax.rem(z + d, n_batch))
                for d in range(1, n_batch)]
    for c in offs_out:
        c.start()

    up = [
        remote(tile_ref.at[:, :ps, :ps], ext.at[:, ts:, :ps], sems(), me - TILE_COLS, z),
        remote(tile_ref.at[:, :ps, ps:], ext.at[:, ts:, ps:ts], sems(), me - TILE_COLS, z),
    ]
    leftward = remote(tile_ref.at[:, :, :ps], ext.at[:, :ts, ts:], sems(), me - 1, z)
    corner = remote(ext.at[:, ts:, :ps], ext.at[:, ts:, ts:], sems(), me - 1, z)

    @pl.when(has_up)
    def _():
        up[0].start()
        up[1].start()

    @pl.when(has_left)
    def _():
        leftward.start()

    ext[:, :ts, :ts] = tile_ref[...]

    @pl.when(jnp.logical_not(has_right))
    def _():
        ext[:, :, ts:] = jnp.zeros((2, ts + ps, ps), F32)

    @pl.when(jnp.logical_not(has_down))
    def _():
        ext[:, ts:, :ts] = jnp.zeros((2, ps, ts), F32)

    @pl.when(jnp.logical_and(jnp.logical_not(has_down), has_right))
    def _():
        ext[:, ts:, ts:] = jnp.zeros((2, ps, ps), F32)

    rows = lax.broadcasted_iota(jnp.int32, (ps, ps), 0)
    cols = lax.broadcasted_iota(jnp.int32, (ps, ps), 1)
    by_row = onehot(cols == jnp.where(rows < h, 2 * rows, 2 * (rows - h) + 1))
    by_col = onehot(rows == jnp.where(cols < h, 2 * cols, 2 * (cols - h) + 1))
    fac[...] = times_onehot(onehot_times(by_row, amp_ref[...]), by_col)

    @pl.when(has_down)
    def _():
        up[0].wait_recv()

    @pl.when(jnp.logical_and(has_down, has_left))
    def _():
        corner.start()

    @pl.when(has_down)
    def _():
        up[1].wait_recv()

    @pl.when(has_right)
    def _():
        leftward.wait_recv()

    @pl.when(jnp.logical_and(has_down, has_right))
    def _():
        corner.wait_recv()

    r_at = off_ref[0:1, 0:1]
    c_at = off_ref[1:2, 0:1]
    te = ts + ps
    pick_r = onehot(lax.broadcasted_iota(jnp.int32, (ps, te), 1)
                    == lax.broadcasted_iota(jnp.int32, (ps, te), 0) + r_at)
    pick_c = onehot(lax.broadcasted_iota(jnp.int32, (te, ps), 0)
                    == lax.broadcasted_iota(jnp.int32, (te, ps), 1) + c_at)
    for part in range(2):
        patch[part] = times_onehot(onehot_times(pick_r, ext[part]), pick_c)

    @pl.when(has_up)
    def _():
        up[0].wait_send()
        up[1].wait_send()

    @pl.when(has_left)
    def _():
        leftward.wait_send()

    @pl.when(jnp.logical_and(has_down, has_left))
    def _():
        corner.wait_send()

    def forward(k, intensity):
        i0, i1 = intensity
        pr, pi = probe_ref[k, 0].astype(F32), probe_ref[k, 1].astype(F32)
        a, b = patch[0], patch[1]
        xr, xi = pr * a - pi * b, pr * b + pi * a
        plus = jnp.concatenate([xr[:, :h] + xr[:, h:], xi[:, :h] + xi[:, h:]], 1)
        minus = jnp.concatenate([xr[:, :h] - xr[:, h:], xi[:, :h] - xi[:, h:]], 1)
        e = times_table(plus, right_ref[0])
        o = times_table(minus, right_ref[1])
        re = jnp.concatenate([e[:, :h], o[:, :h]], 1)
        im = jnp.concatenate([e[:, h:], o[:, h:]], 1)
        g = table_times(left_ref[0], jnp.concatenate([re[:h] + re[h:], im[:h] + im[h:]], 0))
        f = table_times(left_ref[1], jnp.concatenate([re[:h] - re[h:], im[:h] - im[h:]], 0))
        far[k, 0] = g
        far[k, 1] = f
        return (i0 + g[:h] * g[:h] + g[h:] * g[h:], i1 + f[:h] * f[:h] + f[h:] * f[h:])

    zero = jnp.zeros((h, ps), F32)
    i0, i1 = lax.fori_loop(
        0, modes // 2, lambda i, c: forward(2 * i + 1, forward(2 * i, c)), (zero, zero))
    fac[:h] = 1.0 - fac[:h] / jnp.sqrt(i0 + 0.01)
    fac[h:] = 1.0 - fac[h:] / jnp.sqrt(i1 + 0.01)
    ot[...] = jnp.zeros_like(ot)

    def backward(k):
        f0, f1 = fac[:h], fac[h:]
        g = far[k, 0] * jnp.concatenate([f0, f0], 0)
        f = far[k, 1] * jnp.concatenate([f1, f1], 0)
        p = table_times(left_ref[2], g)
        q = table_times(left_ref[3], f)
        top, low = p + q, p - q
        re = jnp.concatenate([top[:h], low[:h]], 0)
        im = jnp.concatenate([top[h:], low[h:]], 0)
        e = times_table(jnp.concatenate([re[:, :h], im[:, :h]], 1), right_ref[2])
        o = times_table(jnp.concatenate([re[:, h:], im[:, h:]], 1), right_ref[3])
        br = jnp.concatenate([e[:, :h] + o[:, :h], e[:, :h] - o[:, :h]], 1)
        bi = jnp.concatenate([e[:, h:] + o[:, h:], e[:, h:] - o[:, h:]], 1)
        pr, pi = probe_ref[k, 0].astype(F32), probe_ref[k, 1].astype(F32)
        ot[0] += pr * br + pi * bi
        ot[1] += pr * bi - pi * br
        a, b = patch[0], patch[1]
        return a * br + b * bi, a * bi - b * br

    mode_rows = 2 * ps
    pair = sems(mh)

    def pair_copy(i):
        at = pl.ds(pl.multiple_of(i * mode_rows, mode_rows), mode_rows)
        return remote(sendbuf.at[at], pairbuf.at[at], pair + i, sibling, z)

    def both(i):
        gr, gi = backward((1 - core) * mh + i)
        at = pl.multiple_of(i * mode_rows, mode_rows)
        sendbuf[pl.ds(at, ps)] = gr
        sendbuf[pl.ds(at + ps, ps)] = gi
        pair_copy(i).start()
        gr, gi = backward(core * mh + i)
        pair_copy(i).wait_recv()
        acc[pl.ds(at, ps)] = gr + pairbuf[pl.ds(at, ps)]
        acc[pl.ds(at + ps, ps)] = gi + pairbuf[pl.ds(at + ps, ps)]

    n_streams = streams_of(n_tile, n_batch, mh, mode_rows)
    length = mh * mode_rows // n_streams
    per_stream = mh // n_streams
    stream_sems = 2 * len(bits) + 2 * n_batch + 1
    base_out = core * (mh * mode_rows)

    class Stream:
        def __init__(self, index, order):
            self.index, self.order = index, order
            self.first = index * length
            self.start, self.size, self.step = self.first, length, 0
            self.slot = 0
            self.sem_rs = stream_base + index * stream_sems
            self.sem_ag = self.sem_rs + len(order)
            self.sem_z = self.sem_ag + len(order)
            self.sem_zg = self.sem_z + n_batch
            self.sem_pair = self.sem_zg + n_batch
            self.trail = []

        def rows(self, at, n):
            return pl.ds(pl.multiple_of(at, n), n)

        def rs_start(self):
            b = self.order[self.step]
            mine = lax.rem(me // b, 2)
            half = self.size // 2
            self.partner = me + b * (1 - 2 * mine)
            self.trail.append((self.start, self.size, self.partner, mine))
            self.copy = remote(
                acc.at[self.rows(self.start + (1 - mine) * half, half)],
                rsbuf.at[self.index, pl.ds(self.slot, half)],
                self.sem_rs + self.step, self.partner, z)
            if self.step:
                self.copy.start()
            self.start = self.start + mine * half
            self.size = half

        def rs_wait(self):
            self.copy.wait()
            at = self.rows(self.start, self.size)
            acc[at] += rsbuf[self.index, self.slot:self.slot + self.size]
            self.slot += self.size
            self.step += 1

        def z_start(self):
            q = self.size // n_batch
            self.q = q
            self.copies = []
            for d in range(1, n_batch):
                dest = lax.rem(z + d, n_batch)
                c = remote(acc.at[self.rows(self.start + dest * q, q)], zbuf.at[self.index, d],
                           self.sem_z + d, me, dest)
                c.start()
                self.copies.append(c)

        def z_wait(self):
            for c in self.copies:
                c.wait()
            total = acc[self.rows(self.start + z * self.q, self.q)]
            for d in range(1, n_batch):
                total = total + zbuf[self.index, d]
            at = self.rows(base_out + self.start + z * self.q, self.q)
            pg_ref[at] = total
            self.copies = []
            for d in range(1, n_batch):
                c = remote(pg_ref.at[at], pg_ref.at[at], self.sem_zg + d, me, lax.rem(z + d, n_batch))
                c.start()
                self.copies.append(c)

        def zg_wait(self):
            for c in self.copies:
                c.wait()

        def ag_start(self):
            self.step -= 1
            start, size, partner, mine = self.trail[self.step]
            at = self.rows(base_out + start + mine * (size // 2), size // 2)
            self.copy = remote(pg_ref.at[at], pg_ref.at[at], self.sem_ag + self.step, partner, z)
            self.copy.start()

        def ag_wait(self):
            self.copy.wait()

        def pair_start(self):
            at = self.rows(base_out + self.first, length)
            self.copy = remote(pg_ref.at[at], pg_ref.at[at], self.sem_pair, sibling, z)
            self.copy.start()

    stream_base = sems(n_streams * stream_sems)

    def summed(i, carry):
        for j in range(per_stream):
            both(i * per_stream + j)
        bit = bits[0] + lax.rem(i, 2) * (bits[-1] - bits[0])
        mine = lax.rem(me // bit, 2)
        half = length // 2
        at = pl.multiple_of(i * length + (1 - mine) * half, half)
        remote(acc.at[pl.ds(at, half)], rsbuf.at[i, pl.ds(0, half)],
               stream_base + i * stream_sems, me + bit * (1 - 2 * mine), z).start()
        return carry

    lax.fori_loop(0, n_streams, summed, 0)
    streams = [Stream(i, bits if i % 2 == 0 else bits[::-1]) for i in range(n_streams)]
    for s in streams:
        s.rs_start()

    osem = sems(4 * n_batch)
    hops = n_batch - 1

    def sem_of(way, stage, part):
        return osem + stage + n_batch * (2 * part + (1 if way < 0 else 0))

    def passing(way, stage, part):
        origin = z - way * stage
        sends = jnp.logical_and(
            jnp.logical_and(origin >= 0, origin < n_batch),
            jnp.logical_and(z + way >= 0, z + way < n_batch))
        at = jnp.clip(origin, 0, n_batch - 1)
        src = ot.at[part] if stage == 0 else objbuf.at[at, part]
        to = jnp.clip(z + way, 0, n_batch - 1)
        return sends, remote(src, objbuf.at[at, part], sem_of(way, stage, part), me, to)

    def arrival(way, stage, part):
        origin = z - way * (1 + stage)
        comes = jnp.logical_and(origin >= 0, origin < n_batch)
        at = jnp.clip(origin, 0, n_batch - 1)
        return comes, at, remote(ot.at[part], objbuf.at[at, part], sem_of(way, stage, part),
                                 me, jnp.clip(z + way, 0, n_batch - 1))

    def start_passing(stage, part):
        for way in (1, -1):
            sends, c = passing(way, stage, part)

            @pl.when(sends)
            def _():
                c.start()

    def place(offs, term):
        put_r = onehot(lax.broadcasted_iota(jnp.int32, (te, ps), 0)
                       == lax.broadcasted_iota(jnp.int32, (te, ps), 1) + offs[0:1, 0:1])
        put_c = onehot(lax.broadcasted_iota(jnp.int32, (ps, te), 1)
                       == lax.broadcasted_iota(jnp.int32, (ps, te), 0) + offs[1:2, 0:1])
        return onehot_times(put_r, times_onehot(term, put_c))

    right_sem, down_sem = sems(2), sems(2)
    rightward = [remote(gext.at[part, :, ts:], xbuf.at[part], right_sem + part, me + 1, z)
                 for part in range(2)]
    downward = [remote(gext.at[part, ts:, :ts], ybuf.at[part], down_sem + part, me + TILE_COLS, z)
                for part in range(2)]

    def arrived(stage, part):
        for way in (1, -1):
            comes, at, c = arrival(way, stage, part)

            @pl.when(comes)
            def _():
                c.wait_recv()
        if stage + 1 < hops:
            start_passing(stage + 1, part)
        if part == 0 and stage == max(hops - 2, 0):
            start_passing(0, 1)
        for way in (1, -1):
            comes, at, c = arrival(way, stage, part)
            slot = stage + 1 if way > 0 else n_batch - 1 - stage

            @pl.when(comes)
            def _():
                gext[part] += place(offbuf.at[slot], objbuf[at, part])

        if stage + 1 == hops:
            @pl.when(has_right)
            def _():
                rightward[part].start()

    def margin(part):
        @pl.when(has_left)
        def _():
            rightward[part].wait_recv()
            gext[part, :, :ps] += xbuf[part]

        @pl.when(has_down)
        def _():
            downward[part].start()

    start_passing(0, 0)
    for part in range(2):
        gext[part] = place(off_ref, ot[part])
    for c in offs_out:
        c.wait()

    todo = [functools.partial(arrived, stage, part) for part in range(2) for stage in range(hops)]

    def serve():
        if todo:
            todo.pop(0)()

    for step in range(len(bits)):
        serve()
        for s in streams:
            s.rs_wait()
            if step + 1 < len(bits):
                s.rs_start()
            else:
                s.z_start()
    while len(todo) > hops:
        serve()
    serve()
    for s in streams:
        s.z_wait()
    while len(todo) > 1:
        serve()
    margin(0)
    for s in streams:
        s.zg_wait()
        s.ag_start()
    serve()
    for step in range(len(bits)):
        for s in streams:
            s.ag_wait()
            if step + 1 < len(bits):
                s.ag_start()
            else:
                s.pair_start()
        if step == 0:
            margin(1)

    for part in range(2):
        og_ref[part] = gext[part, :ts, :ts]

        @pl.when(has_up)
        def _():
            downward[part].wait_recv()
            og_ref[part, :ps, :] += ybuf[part]

    for part in range(2):
        @pl.when(has_right)
        def _():
            rightward[part].wait_send()

        @pl.when(has_down)
        def _():
            downward[part].wait_send()

    for s in streams:
        s.copy.wait()

    for part in range(2):
        for stage in range(hops):
            for way in (1, -1):
                sends, c = passing(way, stage, part)

                @pl.when(sends)
                def _():
                    c.wait_send()

    def sent(i, carry):
        pair_copy(i).wait_send()
        return carry

    lax.fori_loop(0, mh, sent, 0)


def streams_of(n_tile, n_batch, mh, mode_rows):
    return mh if mode_rows // (n_tile // 2) // n_batch >= 8 else 2


def n_sems(n_tile, n_batch, mh, n_streams):
    n_bits = n_tile.bit_length() - 2
    return 4 + mh + n_streams * (2 * n_bits + 2 * n_batch + 1) + 5 * n_batch + 4


def shards(n_tile, n_batch, object_tiles, probe, offsets, amplitude):
    modes, _, ps, _ = probe.shape
    ts = object_tiles.shape[-1]
    te = ts + ps
    rights, lefts = dft_tables(ps)
    held = jnp.broadcast_to(jnp.pad(offsets[0, 0], (0, 6))[:, None], (8, 128))
    n_streams = streams_of(n_tile, n_batch, modes // 2, 2 * ps)
    n = n_sems(n_tile, n_batch, modes // 2, n_streams)
    half = modes // 2 * 2 * ps
    length = half // n_streams
    q = length // (n_tile // 2) // n_batch
    vmem = pl.BlockSpec(memory_space=pltpu.VMEM)
    og, pg = pl.pallas_call(
        functools.partial(kernel, n_tile, n_batch),
        out_shape=(jax.ShapeDtypeStruct((2, ts, ts), F32),
                   jax.ShapeDtypeStruct((modes * 2 * ps, ps), F32)),
        in_specs=[vmem] * 6,
        out_specs=(vmem, vmem),
        scratch_shapes=[
            pltpu.VMEM((2, te, te), F32),
            pltpu.VMEM((2, ps, ps), F32),
            pltpu.VMEM((modes, 2, ps, ps), F32),
            pltpu.VMEM((ps, ps), F32),
            pltpu.VMEM((2, ps, ps), F32),
            pltpu.VMEM((2, te, te), F32),
            pltpu.VMEM((half, ps), F32),
            pltpu.VMEM((half, ps), F32),
            pltpu.VMEM((half, ps), F32),
            pltpu.VMEM((n_streams, length, ps), F32),
            pltpu.VMEM((n_streams, n_batch, q, ps), F32),
            pltpu.VMEM((n_batch, 2, ps, ps), F32),
            pltpu.VMEM((n_batch, 8, 128), jnp.int32),
            pltpu.VMEM((2, te, ps), F32),
            pltpu.VMEM((2, ps, ts), F32),
            pltpu.SemaphoreType.DMA((n,)),
            pltpu.SemaphoreType.DMA((n,)),
        ],
        compiler_params=pltpu.CompilerParams(
            collective_id=0, has_side_effects=True, vmem_limit_bytes=56 * 1024 * 1024),
        cost_estimate=pl.CostEstimate(flops=13_000_000_000, bytes_accessed=20_000_000, transcendentals=0),
        name="ptycho",
    )(object_tiles[0], held, amplitude[0, 0], probe, rights, lefts)
    positions = n_tile * n_batch * offsets.shape[1]
    return og[None], pg.reshape(modes, 2, ps, ps) * (1.0 / math.sqrt(positions))


def solution(mesh):
    placed = (
        P("tile", None, None, None),
        P(),
        P("tile", "batch", None),
        P("tile", "batch", None, None),
    )
    return jax.shard_map(
        functools.partial(shards, mesh.shape["tile"], mesh.shape["batch"]),
        mesh=mesh,
        in_specs=placed,
        out_specs=(P("tile", None, None, None), P()),
        check_vma=False,
    )
```

```python
import functools
import math

import jax
import jax.numpy as jnp
import ml_dtypes
import numpy as np
from jax import lax
from jax.experimental import pallas as pl
from jax.experimental.pallas import tpu as pltpu
from jax.sharding import PartitionSpec as P

TILE_COLS = 4
MESH = pl.DeviceIdType.MESH
F32 = jnp.float32
BF16 = jnp.bfloat16


def split_table(table, axis):
    high = table.astype(np.float32).astype(ml_dtypes.bfloat16)
    low = (table - high.astype(np.float64)).astype(np.float32).astype(ml_dtypes.bfloat16)
    return np.concatenate([high, high, low], axis=axis)


def dft_tables(pattern):
    h = pattern // 2
    n, k = np.arange(h)[:, None], np.arange(h)[None, :]
    even = np.exp(-2j * np.pi * ((2 * n * k) % pattern) / pattern) / math.sqrt(pattern)
    odd = np.exp(-2j * np.pi * ((n * (2 * k + 1)) % pattern) / pattern) / math.sqrt(pattern)

    def right(m):
        return split_table(np.block([[m.real, m.imag], [-m.imag, m.real]]), 0)

    def left(m):
        return split_table(np.block([[m.real, -m.imag], [m.imag, m.real]]), 1)

    rights = np.stack([right(even), right(odd), right(even.conj().T), right(odd.conj().T)])
    lefts = np.stack([left(even.T), left(odd.T), left(even.conj()), left(odd.conj())])
    return rights, lefts


def split(x):
    high = x.astype(BF16)
    return high, (x - high.astype(F32)).astype(BF16)


def times_table(x, table):
    high, low = split(x)
    return jnp.dot(jnp.concatenate([high, low, high], 1), table, preferred_element_type=F32)


def table_times(table, x):
    high, low = split(x)
    return jnp.dot(table, jnp.concatenate([high, low, high], 0), preferred_element_type=F32)


def times_onehot(x, onehot):
    high, low = split(x)
    return jnp.dot(high, onehot, preferred_element_type=F32) + jnp.dot(
        low, onehot, preferred_element_type=F32
    )


def onehot_times(onehot, x):
    high, low = split(x)
    return jnp.dot(onehot, high, preferred_element_type=F32) + jnp.dot(
        onehot, low, preferred_element_type=F32
    )


def onehot(hit):
    return jnp.where(hit, 1.0, 0.0).astype(F32).astype(BF16)


def kernel(n_tile, n_batch, tile_ref, off_ref, amp_ref, probe_ref, right_ref, left_ref,
           og_ref, pg_ref, ext, patch, far, fac, ot, gext, acc, sendbuf, pairbuf, rsbuf, zbuf, zfbuf,
           objbuf, offbuf, xbuf, ybuf, send_sem, recv_sem):
    me = lax.axis_index("tile")
    z = lax.axis_index("batch")
    ts = tile_ref.shape[-1]
    modes, _, ps, _ = probe_ref.shape
    h = ps // 2
    mh = modes // 2
    bits = []
    b = 2
    while b < n_tile:
        bits.append(b)
        b *= 2
    core = lax.rem(me, 2)
    sibling = me + 1 - 2 * core
    col = lax.rem(me, TILE_COLS)
    has_left = col > 0
    has_right = col < TILE_COLS - 1
    has_up = me >= TILE_COLS
    has_down = me < n_tile - TILE_COLS
    count = [0]

    def sems(n=1):
        first = count[0]
        count[0] += n
        return first

    def remote(src, dst, sem, tile, batch):
        return pltpu.make_async_remote_copy(
            src_ref=src, dst_ref=dst, send_sem=send_sem.at[sem], recv_sem=recv_sem.at[sem],
            device_id=(tile, batch), device_id_type=MESH)

    barrier = pltpu.get_barrier_semaphore()

    def greet(tile, batch):
        pl.semaphore_signal(barrier, inc=1, device_id=(tile, batch), device_id_type=MESH)

    greet(sibling, z)
    for b in bits:
        greet(me + b * (1 - 2 * lax.rem(me // b, 2)), z)
    for d in range(1, n_batch):
        greet(me, lax.rem(z + d, n_batch))
    for there, step in ((has_left, -1), (has_right, 1), (has_up, -TILE_COLS), (has_down, TILE_COLS)):
        @pl.when(there)
        def _():
            greet(me + step, z)
    around = sum(jnp.where(t, 1, 0) for t in (has_left, has_right, has_up, has_down))
    pl.semaphore_wait(barrier, 1 + len(bits) + n_batch - 1 + around)

    fsem = sems(n_batch)
    offs_out = [remote(off_ref, offbuf.at[d], fsem + d, me, lax.rem(z + d, n_batch))
                for d in range(1, n_batch)]
    for c in offs_out:
        c.start()

    own = lax.rem(z, 2)
    twin = z + 1 - 2 * own
    pieces = (slice(0, ps), slice(ps, ts))
    up = [remote(tile_ref.at[own, :ps, c], ext.at[own, ts:, c], sems(), me - TILE_COLS, z)
          for c in pieces]
    share = [remote(ext.at[own, ts:, c], ext.at[own, ts:, c], sems(), me, twin) for c in pieces]
    leftward = remote(tile_ref.at[:, :, :ps], ext.at[:, :ts, ts:], sems(), me - 1, z)
    corner = [remote(ext.at[part, ts:, :ps], ext.at[part, ts:, ts:], sems(), me - 1, z)
              for part in (own, 1 - own)]

    @pl.when(has_up)
    def _():
        up[0].start()
        up[1].start()

    @pl.when(has_left)
    def _():
        leftward.start()

    ext[:, :ts, :ts] = tile_ref[...]

    @pl.when(jnp.logical_not(has_right))
    def _():
        ext[:, :, ts:] = jnp.zeros((2, ts + ps, ps), F32)

    @pl.when(jnp.logical_not(has_down))
    def _():
        ext[:, ts:, :ts] = jnp.zeros((2, ps, ts), F32)

    @pl.when(jnp.logical_and(jnp.logical_not(has_down), has_right))
    def _():
        ext[:, ts:, ts:] = jnp.zeros((2, ps, ps), F32)

    rows = lax.broadcasted_iota(jnp.int32, (ps, ps), 0)
    cols = lax.broadcasted_iota(jnp.int32, (ps, ps), 1)
    by_row = onehot(cols == jnp.where(rows < h, 2 * rows, 2 * (rows - h) + 1))
    by_col = onehot(rows == jnp.where(cols < h, 2 * cols, 2 * (cols - h) + 1))
    fac[...] = times_onehot(onehot_times(by_row, amp_ref[...]), by_col)

    @pl.when(has_down)
    def _():
        up[0].wait_recv()
        share[0].start()

    @pl.when(jnp.logical_and(has_down, has_left))
    def _():
        corner[0].start()

    @pl.when(has_down)
    def _():
        up[1].wait_recv()
        share[1].start()
        share[0].wait_recv()

    @pl.when(jnp.logical_and(has_down, has_left))
    def _():
        corner[1].start()

    @pl.when(has_down)
    def _():
        share[1].wait_recv()

    @pl.when(has_right)
    def _():
        leftward.wait_recv()

    @pl.when(jnp.logical_and(has_down, has_right))
    def _():
        corner[0].wait_recv()
        corner[1].wait_recv()

    r_at = off_ref[0:1, 0:1]
    c_at = off_ref[1:2, 0:1]
    te = ts + ps
    pick_r = onehot(lax.broadcasted_iota(jnp.int32, (ps, te), 1)
                    == lax.broadcasted_iota(jnp.int32, (ps, te), 0) + r_at)
    pick_c = onehot(lax.broadcasted_iota(jnp.int32, (te, ps), 0)
                    == lax.broadcasted_iota(jnp.int32, (te, ps), 1) + c_at)
    for part in range(2):
        patch[part] = times_onehot(onehot_times(pick_r, ext[part]), pick_c)

    @pl.when(has_up)
    def _():
        up[0].wait_send()
        up[1].wait_send()

    @pl.when(has_left)
    def _():
        leftward.wait_send()

    @pl.when(jnp.logical_and(has_down, has_left))
    def _():
        corner[0].wait_send()
        corner[1].wait_send()

    @pl.when(has_down)
    def _():
        share[0].wait_send()
        share[1].wait_send()

    def forward(k, intensity):
        i0, i1 = intensity
        pr, pi = probe_ref[k, 0].astype(F32), probe_ref[k, 1].astype(F32)
        a, b = patch[0], patch[1]
        xr, xi = pr * a - pi * b, pr * b + pi * a
        plus = jnp.concatenate([xr[:, :h] + xr[:, h:], xi[:, :h] + xi[:, h:]], 1)
        minus = jnp.concatenate([xr[:, :h] - xr[:, h:], xi[:, :h] - xi[:, h:]], 1)
        e = times_table(plus, right_ref[0])
        o = times_table(minus, right_ref[1])
        re = jnp.concatenate([e[:, :h], o[:, :h]], 1)
        im = jnp.concatenate([e[:, h:], o[:, h:]], 1)
        g = table_times(left_ref[0], jnp.concatenate([re[:h] + re[h:], im[:h] + im[h:]], 0))
        f = table_times(left_ref[1], jnp.concatenate([re[:h] - re[h:], im[:h] - im[h:]], 0))
        far[k, 0] = g
        far[k, 1] = f
        return (i0 + g[:h] * g[:h] + g[h:] * g[h:], i1 + f[:h] * f[:h] + f[h:] * f[h:])

    zero = jnp.zeros((h, ps), F32)
    i0, i1 = lax.fori_loop(
        0, modes // 2, lambda i, c: forward(2 * i + 1, forward(2 * i, c)), (zero, zero))
    fac[:h] = 1.0 - fac[:h] / jnp.sqrt(i0 + 0.01)
    fac[h:] = 1.0 - fac[h:] / jnp.sqrt(i1 + 0.01)
    ot[...] = jnp.zeros_like(ot)

    def backward(k):
        f0, f1 = fac[:h], fac[h:]
        g = far[k, 0] * jnp.concatenate([f0, f0], 0)
        f = far[k, 1] * jnp.concatenate([f1, f1], 0)
        p = table_times(left_ref[2], g)
        q = table_times(left_ref[3], f)
        top, low = p + q, p - q
        re = jnp.concatenate([top[:h], low[:h]], 0)
        im = jnp.concatenate([top[h:], low[h:]], 0)
        e = times_table(jnp.concatenate([re[:, :h], im[:, :h]], 1), right_ref[2])
        o = times_table(jnp.concatenate([re[:, h:], im[:, h:]], 1), right_ref[3])
        br = jnp.concatenate([e[:, :h] + o[:, :h], e[:, :h] - o[:, :h]], 1)
        bi = jnp.concatenate([e[:, h:] + o[:, h:], e[:, h:] - o[:, h:]], 1)
        pr, pi = probe_ref[k, 0].astype(F32), probe_ref[k, 1].astype(F32)
        ot[0] += pr * br + pi * bi
        ot[1] += pr * bi - pi * br
        a, b = patch[0], patch[1]
        return a * br + b * bi, a * bi - b * br

    mode_rows = 2 * ps
    pair = sems(mh)

    def pair_copy(i):
        at = pl.ds(pl.multiple_of(i * mode_rows, mode_rows), mode_rows)
        return remote(sendbuf.at[at], pairbuf.at[at], pair + i, sibling, z)

    def both(i):
        gr, gi = backward((1 - core) * mh + i)
        at = pl.multiple_of(i * mode_rows, mode_rows)
        sendbuf[pl.ds(at, ps)] = gr
        sendbuf[pl.ds(at + ps, ps)] = gi
        pair_copy(i).start()
        gr, gi = backward(core * mh + i)
        pair_copy(i).wait_recv()
        acc[pl.ds(at, ps)] = gr + pairbuf[pl.ds(at, ps)]
        acc[pl.ds(at + ps, ps)] = gi + pairbuf[pl.ds(at + ps, ps)]

    n_streams = streams_of(n_tile, n_batch, mh, mode_rows)
    length = mh * mode_rows // n_streams
    per_stream = mh // n_streams
    stream_sems = 2 * len(bits) + 2 * n_batch + 1
    base_out = core * (mh * mode_rows)

    class Stream:
        def __init__(self, index, order, z_first=False):
            self.index, self.order, self.z_first = index, order, z_first
            self.first = index * length
            self.start, self.size, self.step = self.first, length, 0
            self.slot = 0
            self.sem_rs = stream_base + index * stream_sems
            self.sem_ag = self.sem_rs + len(order)
            self.sem_z = self.sem_ag + len(order)
            self.sem_zg = self.sem_z + n_batch
            self.sem_pair = self.sem_zg + n_batch
            self.trail = []

        def rows(self, at, n):
            return pl.ds(pl.multiple_of(at, n), n)

        def rs_start(self):
            b = self.order[self.step]
            mine = lax.rem(me // b, 2)
            half = self.size // 2
            self.partner = me + b * (1 - 2 * mine)
            self.trail.append((self.start, self.size, self.partner, mine))
            self.copy = remote(
                acc.at[self.rows(self.start + (1 - mine) * half, half)],
                rsbuf.at[self.index, pl.ds(self.slot, half)],
                self.sem_rs + self.step, self.partner, z)
            if self.step or self.z_first:
                self.copy.start()
            self.start = self.start + mine * half
            self.size = half

        def rs_wait(self):
            self.copy.wait()
            at = self.rows(self.start, self.size)
            acc[at] += rsbuf[self.index, self.slot:self.slot + self.size]
            self.slot += self.size
            self.step += 1

        def zf_start(self):
            q = length // n_batch
            self.copies = []
            for d in range(1, n_batch):
                dest = lax.rem(z + d, n_batch)
                c = remote(acc.at[self.rows(self.first + dest * q, q)], zfbuf.at[d],
                           self.sem_z + d, me, dest)
                c.start()
                self.copies.append(c)

        def zf_wait(self):
            for c in self.copies:
                c.wait()
            self.size = length // n_batch
            self.start = self.first + z * self.size
            at = self.rows(self.start, self.size)
            total = acc[at]
            for d in range(1, n_batch):
                total = total + zfbuf[d]
            acc[at] = total

        def settle(self):
            pg_ref[self.rows(base_out + self.start, self.size)] = acc[self.rows(self.start, self.size)]

        def zl_start(self):
            q = length // n_batch
            at = self.rows(base_out + self.first + z * q, q)
            self.copies = []
            for d in range(1, n_batch):
                c = remote(pg_ref.at[at], pg_ref.at[at], self.sem_zg + d, me, lax.rem(z + d, n_batch))
                c.start()
                self.copies.append(c)

        def z_start(self):
            q = self.size // n_batch
            self.q = q
            self.copies = []
            for d in range(1, n_batch):
                dest = lax.rem(z + d, n_batch)
                c = remote(acc.at[self.rows(self.start + dest * q, q)], zbuf.at[self.index, d],
                           self.sem_z + d, me, dest)
                c.start()
                self.copies.append(c)

        def z_wait(self):
            for c in self.copies:
                c.wait()
            total = acc[self.rows(self.start + z * self.q, self.q)]
            for d in range(1, n_batch):
                total = total + zbuf[self.index, d]
            at = self.rows(base_out + self.start + z * self.q, self.q)
            pg_ref[at] = total
            self.copies = []
            for d in range(1, n_batch):
                c = remote(pg_ref.at[at], pg_ref.at[at], self.sem_zg + d, me, lax.rem(z + d, n_batch))
                c.start()
                self.copies.append(c)

        def zg_wait(self):
            for c in self.copies:
                c.wait()

        def ag_start(self):
            self.step -= 1
            start, size, partner, mine = self.trail[self.step]
            at = self.rows(base_out + start + mine * (size // 2), size // 2)
            self.copy = remote(pg_ref.at[at], pg_ref.at[at], self.sem_ag + self.step, partner, z)
            self.copy.start()

        def ag_wait(self):
            self.copy.wait()

        def pair_start(self):
            at = self.rows(base_out + self.first, length)
            self.copy = remote(pg_ref.at[at], pg_ref.at[at], self.sem_pair, sibling, z)
            self.copy.start()

    stream_base = sems(n_streams * stream_sems)

    def summed(i, carry):
        for j in range(per_stream):
            both(i * per_stream + j)
        bit = bits[0] + lax.rem(i, 2) * (bits[-1] - bits[0])
        mine = lax.rem(me // bit, 2)
        half = length // 2
        at = pl.multiple_of(i * length + (1 - mine) * half, half)
        remote(acc.at[pl.ds(at, half)], rsbuf.at[i, pl.ds(0, half)],
               stream_base + i * stream_sems, me + bit * (1 - 2 * mine), z).start()
        return carry

    for j in range(per_stream):
        both(j)
    around_z = Stream(0, bits, True)
    around_z.zf_start()
    lax.fori_loop(1, n_streams, summed, 0)
    streams = [Stream(i, bits if i % 2 == 0 else bits[::-1]) for i in range(1, n_streams)]
    for s in streams:
        s.rs_start()

    osem = sems(4 * n_batch)
    hops = n_batch - 1

    def sem_of(way, stage, part):
        return osem + stage + n_batch * (2 * part + (1 if way < 0 else 0))

    def passing(way, stage, part):
        origin = z - way * stage
        sends = jnp.logical_and(
            jnp.logical_and(origin >= 0, origin < n_batch),
            jnp.logical_and(z + way >= 0, z + way < n_batch))
        at = jnp.clip(origin, 0, n_batch - 1)
        src = ot.at[part] if stage == 0 else objbuf.at[at, part]
        to = jnp.clip(z + way, 0, n_batch - 1)
        return sends, remote(src, objbuf.at[at, part], sem_of(way, stage, part), me, to)

    def arrival(way, stage, part):
        origin = z - way * (1 + stage)
        comes = jnp.logical_and(origin >= 0, origin < n_batch)
        at = jnp.clip(origin, 0, n_batch - 1)
        return comes, at, remote(ot.at[part], objbuf.at[at, part], sem_of(way, stage, part),
                                 me, jnp.clip(z + way, 0, n_batch - 1))

    def start_passing(stage, part):
        for way in (1, -1):
            sends, c = passing(way, stage, part)

            @pl.when(sends)
            def _():
                c.start()

    def place(offs, term):
        put_r = onehot(lax.broadcasted_iota(jnp.int32, (te, ps), 0)
                       == lax.broadcasted_iota(jnp.int32, (te, ps), 1) + offs[0:1, 0:1])
        put_c = onehot(lax.broadcasted_iota(jnp.int32, (ps, te), 1)
                       == lax.broadcasted_iota(jnp.int32, (ps, te), 0) + offs[1:2, 0:1])
        return onehot_times(put_r, times_onehot(term, put_c))

    right_sem, down_sem = sems(2), sems(2)
    rightward = [remote(gext.at[part, :, ts:], xbuf.at[part], right_sem + part, me + 1, z)
                 for part in range(2)]
    downward = [remote(gext.at[part, ts:, :ts], ybuf.at[part], down_sem + part, me + TILE_COLS, z)
                for part in range(2)]

    def arrived(stage, part):
        for way in (1, -1):
            comes, at, c = arrival(way, stage, part)

            @pl.when(comes)
            def _():
                c.wait_recv()
        if stage + 1 < hops:
            start_passing(stage + 1, part)
        if part == 0 and stage == max(hops - 2, 0):
            start_passing(0, 1)
        for way in (1, -1):
            comes, at, c = arrival(way, stage, part)
            slot = stage + 1 if way > 0 else n_batch - 1 - stage

            @pl.when(comes)
            def _():
                gext[part] += place(offbuf.at[slot], objbuf[at, part])

        if stage + 1 == hops:
            @pl.when(has_right)
            def _():
                rightward[part].start()

    def margin(part):
        @pl.when(has_left)
        def _():
            rightward[part].wait_recv()
            gext[part, :, :ps] += xbuf[part]

        @pl.when(has_down)
        def _():
            downward[part].start()

    start_passing(0, 0)
    for part in range(2):
        gext[part] = place(off_ref, ot[part])
    for c in offs_out:
        c.wait()

    todo = [functools.partial(arrived, stage, part) for part in range(2) for stage in range(hops)]

    def serve():
        if todo:
            todo.pop(0)()

    for step in range(len(bits)):
        serve()
        if step == 0:
            around_z.zf_wait()
        else:
            around_z.rs_wait()
        around_z.rs_start()
        for s in streams:
            s.rs_wait()
            if step + 1 < len(bits):
                s.rs_start()
            else:
                s.z_start()
    while len(todo) > hops:
        serve()
    around_z.rs_wait()
    around_z.settle()
    around_z.ag_start()
    serve()
    for s in streams:
        s.z_wait()
    while len(todo) > 1:
        serve()
    for step in range(len(bits) - 1):
        around_z.ag_wait()
        around_z.ag_start()
    margin(0)
    for s in streams:
        s.zg_wait()
        s.ag_start()
    serve()
    around_z.ag_wait()
    around_z.zl_start()
    for step in range(len(bits)):
        for s in streams:
            s.ag_wait()
            if step + 1 < len(bits):
                s.ag_start()
            else:
                s.pair_start()
        if step == 0:
            margin(1)
    around_z.zg_wait()
    around_z.pair_start()

    for part in range(2):
        og_ref[part] = gext[part, :ts, :ts]

        @pl.when(has_up)
        def _():
            downward[part].wait_recv()
            og_ref[part, :ps, :] += ybuf[part]

    for part in range(2):
        @pl.when(has_right)
        def _():
            rightward[part].wait_send()

        @pl.when(has_down)
        def _():
            downward[part].wait_send()

    for s in [*streams, around_z]:
        s.copy.wait()

    for part in range(2):
        for stage in range(hops):
            for way in (1, -1):
                sends, c = passing(way, stage, part)

                @pl.when(sends)
                def _():
                    c.wait_send()

    def sent(i, carry):
        pair_copy(i).wait_send()
        return carry

    lax.fori_loop(0, mh, sent, 0)


def streams_of(n_tile, n_batch, mh, mode_rows):
    return mh if mode_rows // (n_tile // 2) // n_batch >= 8 else 2


def n_sems(n_tile, n_batch, mh, n_streams):
    n_bits = n_tile.bit_length() - 2
    return 7 + mh + n_streams * (2 * n_bits + 2 * n_batch + 1) + 5 * n_batch + 4


def shards(n_tile, n_batch, object_tiles, probe, offsets, amplitude):
    modes, _, ps, _ = probe.shape
    ts = object_tiles.shape[-1]
    te = ts + ps
    rights, lefts = dft_tables(ps)
    held = jnp.broadcast_to(jnp.pad(offsets[0, 0], (0, 6))[:, None], (8, 128))
    n_streams = streams_of(n_tile, n_batch, modes // 2, 2 * ps)
    n = n_sems(n_tile, n_batch, modes // 2, n_streams)
    half = modes // 2 * 2 * ps
    length = half // n_streams
    q = length // (n_tile // 2) // n_batch
    vmem = pl.BlockSpec(memory_space=pltpu.VMEM)
    og, pg = pl.pallas_call(
        functools.partial(kernel, n_tile, n_batch),
        out_shape=(jax.ShapeDtypeStruct((2, ts, ts), F32),
                   jax.ShapeDtypeStruct((modes * 2 * ps, ps), F32)),
        in_specs=[vmem] * 6,
        out_specs=(vmem, vmem),
        scratch_shapes=[
            pltpu.VMEM((2, te, te), F32),
            pltpu.VMEM((2, ps, ps), F32),
            pltpu.VMEM((modes, 2, ps, ps), F32),
            pltpu.VMEM((ps, ps), F32),
            pltpu.VMEM((2, ps, ps), F32),
            pltpu.VMEM((2, te, te), F32),
            pltpu.VMEM((half, ps), F32),
            pltpu.VMEM((half, ps), F32),
            pltpu.VMEM((half, ps), F32),
            pltpu.VMEM((n_streams, length, ps), F32),
            pltpu.VMEM((n_streams, n_batch, q, ps), F32),
            pltpu.VMEM((n_batch, length // n_batch, ps), F32),
            pltpu.VMEM((n_batch, 2, ps, ps), F32),
            pltpu.VMEM((n_batch, 8, 128), jnp.int32),
            pltpu.VMEM((2, te, ps), F32),
            pltpu.VMEM((2, ps, ts), F32),
            pltpu.SemaphoreType.DMA((n,)),
            pltpu.SemaphoreType.DMA((n,)),
        ],
        compiler_params=pltpu.CompilerParams(
            collective_id=0, has_side_effects=True, vmem_limit_bytes=56 * 1024 * 1024),
        cost_estimate=pl.CostEstimate(flops=13_000_000_000, bytes_accessed=20_000_000, transcendentals=0),
        name="ptycho",
    )(object_tiles[0], held, amplitude[0, 0], probe, rights, lefts)
    positions = n_tile * n_batch * offsets.shape[1]
    return og[None], pg.reshape(modes, 2, ps, ps) * (1.0 / math.sqrt(positions))


def solution(mesh):
    placed = (
        P("tile", None, None, None),
        P(),
        P("tile", "batch", None),
        P("tile", "batch", None, None),
    )
    return jax.shard_map(
        functools.partial(shards, mesh.shape["tile"], mesh.shape["batch"]),
        mesh=mesh,
        in_specs=placed,
        out_specs=(P("tile", None, None, None), P()),
        check_vma=False,
    )
```

```python
import functools
import math

import jax
import jax.numpy as jnp
import ml_dtypes
import numpy as np
from jax import lax
from jax.experimental import pallas as pl
from jax.experimental.pallas import tpu as pltpu
from jax.sharding import PartitionSpec as P

TILE_COLS = 4
MESH = pl.DeviceIdType.MESH
F32 = jnp.float32
BF16 = jnp.bfloat16


def split_table(table, axis):
    high = table.astype(np.float32).astype(ml_dtypes.bfloat16)
    low = (table - high.astype(np.float64)).astype(np.float32).astype(ml_dtypes.bfloat16)
    return np.concatenate([high, high, low], axis=axis)


def dft_tables(pattern):
    h = pattern // 2
    n, k = np.arange(h)[:, None], np.arange(h)[None, :]
    even = np.exp(-2j * np.pi * ((2 * n * k) % pattern) / pattern) / math.sqrt(pattern)
    odd = np.exp(-2j * np.pi * ((n * (2 * k + 1)) % pattern) / pattern) / math.sqrt(pattern)

    def right(m):
        return split_table(np.block([[m.real, m.imag], [-m.imag, m.real]]), 0)

    def left(m):
        return split_table(np.block([[m.real, -m.imag], [m.imag, m.real]]), 1)

    rights = np.stack([right(even), right(odd), right(even.conj().T), right(odd.conj().T)])
    lefts = np.stack([left(even.T), left(odd.T), left(even.conj()), left(odd.conj())])
    return rights, lefts


def split(x):
    high = x.astype(BF16)
    return high, (x - high.astype(F32)).astype(BF16)


def times_table(x, table):
    high, low = split(x)
    return jnp.dot(jnp.concatenate([high, low, high], 1), table, preferred_element_type=F32)


def table_times(table, x):
    high, low = split(x)
    return jnp.dot(table, jnp.concatenate([high, low, high], 0), preferred_element_type=F32)


def times_onehot(x, onehot):
    high, low = split(x)
    return jnp.dot(high, onehot, preferred_element_type=F32) + jnp.dot(
        low, onehot, preferred_element_type=F32
    )


def onehot_times(onehot, x):
    high, low = split(x)
    return jnp.dot(onehot, high, preferred_element_type=F32) + jnp.dot(
        onehot, low, preferred_element_type=F32
    )


def onehot(hit):
    return jnp.where(hit, 1.0, 0.0).astype(F32).astype(BF16)


def kernel(n_tile, n_batch, tile_ref, offsets_ref, amp_hbm, probe_hbm, right_hbm, left_hbm,
           og_hbm, pg_hbm, amp_ref, probe_ref, right_ref, left_ref, off_ref, og_ref, pg_ref, ext, patch, far, fac, ot, gext, acc, sendbuf, pairbuf, rsbuf, zbuf, zfbuf,
           objbuf, offbuf, xbuf, ybuf, send_sem, recv_sem, load_sem,
           out_sem):
    me = lax.axis_index("tile")
    z = lax.axis_index("batch")
    ts = tile_ref.shape[-1]
    modes, _, ps, _ = probe_ref.shape
    h = ps // 2
    mh = modes // 2
    bits = []
    b = 2
    while b < n_tile:
        bits.append(b)
        b *= 2
    core = lax.rem(me, 2)
    sibling = me + 1 - 2 * core
    col = lax.rem(me, TILE_COLS)
    has_left = col > 0
    has_right = col < TILE_COLS - 1
    has_up = me >= TILE_COLS
    has_down = me < n_tile - TILE_COLS
    count = [0]

    def sems(n=1):
        first = count[0]
        count[0] += n
        return first

    def remote(src, dst, sem, tile, batch):
        return pltpu.make_async_remote_copy(
            src_ref=src, dst_ref=dst, send_sem=send_sem.at[sem], recv_sem=recv_sem.at[sem],
            device_id=(tile, batch), device_id_type=MESH)

    loads = [pltpu.make_async_copy(src, dst, load_sem.at[i]) for i, (src, dst) in enumerate(
        ((amp_hbm, amp_ref), (probe_hbm, probe_ref), (right_hbm, right_ref), (left_hbm, left_ref)))]
    for c in loads:
        c.start()
    off_ref[...] = jnp.where(lax.broadcasted_iota(jnp.int32, off_ref.shape, 0) == 0,
                             offsets_ref[0, 0, 0], offsets_ref[0, 0, 1])

    barrier = pltpu.get_barrier_semaphore()

    def greet(tile, batch):
        pl.semaphore_signal(barrier, inc=1, device_id=(tile, batch), device_id_type=MESH)

    greet(sibling, z)
    for b in bits:
        greet(me + b * (1 - 2 * lax.rem(me // b, 2)), z)
    for d in range(1, n_batch):
        greet(me, lax.rem(z + d, n_batch))
    for there, step in ((has_left, -1), (has_right, 1), (has_up, -TILE_COLS), (has_down, TILE_COLS)):
        @pl.when(there)
        def _():
            greet(me + step, z)
    around = sum(jnp.where(t, 1, 0) for t in (has_left, has_right, has_up, has_down))
    pl.semaphore_wait(barrier, 1 + len(bits) + n_batch - 1 + around)

    fsem = sems(n_batch)
    offs_out = [remote(off_ref, offbuf.at[d], fsem + d, me, lax.rem(z + d, n_batch))
                for d in range(1, n_batch)]
    for c in offs_out:
        c.start()

    own = lax.rem(z, 2)
    twin = z + 1 - 2 * own
    pieces = (slice(0, ps), slice(ps, ts))
    up = [remote(tile_ref.at[own, :ps, c], ext.at[own, ts:, c], sems(), me - TILE_COLS, z)
          for c in pieces]
    share = [remote(ext.at[own, ts:, c], ext.at[own, ts:, c], sems(), me, twin) for c in pieces]
    leftward = remote(tile_ref.at[:, :, :ps], ext.at[:, :ts, ts:], sems(), me - 1, z)
    corner = [remote(ext.at[part, ts:, :ps], ext.at[part, ts:, ts:], sems(), me - 1, z)
              for part in (own, 1 - own)]

    @pl.when(has_up)
    def _():
        up[0].start()
        up[1].start()

    @pl.when(has_left)
    def _():
        leftward.start()

    ext[:, :ts, :ts] = tile_ref[...]

    @pl.when(jnp.logical_not(has_right))
    def _():
        ext[:, :, ts:] = jnp.zeros((2, ts + ps, ps), F32)

    @pl.when(jnp.logical_not(has_down))
    def _():
        ext[:, ts:, :ts] = jnp.zeros((2, ps, ts), F32)

    @pl.when(jnp.logical_and(jnp.logical_not(has_down), has_right))
    def _():
        ext[:, ts:, ts:] = jnp.zeros((2, ps, ps), F32)

    loads[0].wait()
    rows = lax.broadcasted_iota(jnp.int32, (ps, ps), 0)
    cols = lax.broadcasted_iota(jnp.int32, (ps, ps), 1)
    by_row = onehot(cols == jnp.where(rows < h, 2 * rows, 2 * (rows - h) + 1))
    by_col = onehot(rows == jnp.where(cols < h, 2 * cols, 2 * (cols - h) + 1))
    fac[...] = times_onehot(onehot_times(by_row, amp_ref[...]), by_col)

    @pl.when(has_down)
    def _():
        up[0].wait_recv()
        share[0].start()

    @pl.when(jnp.logical_and(has_down, has_left))
    def _():
        corner[0].start()

    @pl.when(has_down)
    def _():
        up[1].wait_recv()
        share[1].start()
        share[0].wait_recv()

    @pl.when(jnp.logical_and(has_down, has_left))
    def _():
        corner[1].start()

    @pl.when(has_down)
    def _():
        share[1].wait_recv()

    @pl.when(has_right)
    def _():
        leftward.wait_recv()

    @pl.when(jnp.logical_and(has_down, has_right))
    def _():
        corner[0].wait_recv()
        corner[1].wait_recv()

    r_at = off_ref[0:1, 0:1]
    c_at = off_ref[1:2, 0:1]
    te = ts + ps
    pick_r = onehot(lax.broadcasted_iota(jnp.int32, (ps, te), 1)
                    == lax.broadcasted_iota(jnp.int32, (ps, te), 0) + r_at)
    pick_c = onehot(lax.broadcasted_iota(jnp.int32, (te, ps), 0)
                    == lax.broadcasted_iota(jnp.int32, (te, ps), 1) + c_at)
    for part in range(2):
        patch[part] = times_onehot(onehot_times(pick_r, ext[part]), pick_c)

    @pl.when(has_up)
    def _():
        up[0].wait_send()
        up[1].wait_send()

    @pl.when(has_left)
    def _():
        leftward.wait_send()

    @pl.when(jnp.logical_and(has_down, has_left))
    def _():
        corner[0].wait_send()
        corner[1].wait_send()

    @pl.when(has_down)
    def _():
        share[0].wait_send()
        share[1].wait_send()

    for c in loads[1:]:
        c.wait()

    def forward(k, intensity):
        i0, i1 = intensity
        pr, pi = probe_ref[k, 0].astype(F32), probe_ref[k, 1].astype(F32)
        a, b = patch[0], patch[1]
        xr, xi = pr * a - pi * b, pr * b + pi * a
        plus = jnp.concatenate([xr[:, :h] + xr[:, h:], xi[:, :h] + xi[:, h:]], 1)
        minus = jnp.concatenate([xr[:, :h] - xr[:, h:], xi[:, :h] - xi[:, h:]], 1)
        e = times_table(plus, right_ref[0])
        o = times_table(minus, right_ref[1])
        re = jnp.concatenate([e[:, :h], o[:, :h]], 1)
        im = jnp.concatenate([e[:, h:], o[:, h:]], 1)
        g = table_times(left_ref[0], jnp.concatenate([re[:h] + re[h:], im[:h] + im[h:]], 0))
        f = table_times(left_ref[1], jnp.concatenate([re[:h] - re[h:], im[:h] - im[h:]], 0))
        far[k, 0] = g
        far[k, 1] = f
        return (i0 + g[:h] * g[:h] + g[h:] * g[h:], i1 + f[:h] * f[:h] + f[h:] * f[h:])

    zero = jnp.zeros((h, ps), F32)
    i0, i1 = lax.fori_loop(
        0, modes // 2, lambda i, c: forward(2 * i + 1, forward(2 * i, c)), (zero, zero))
    fac[:h] = 1.0 - fac[:h] / jnp.sqrt(i0 + 0.01)
    fac[h:] = 1.0 - fac[h:] / jnp.sqrt(i1 + 0.01)
    ot[...] = jnp.zeros_like(ot)

    def backward(k):
        f0, f1 = fac[:h], fac[h:]
        g = far[k, 0] * jnp.concatenate([f0, f0], 0)
        f = far[k, 1] * jnp.concatenate([f1, f1], 0)
        p = table_times(left_ref[2], g)
        q = table_times(left_ref[3], f)
        top, low = p + q, p - q
        re = jnp.concatenate([top[:h], low[:h]], 0)
        im = jnp.concatenate([top[h:], low[h:]], 0)
        e = times_table(jnp.concatenate([re[:, :h], im[:, :h]], 1), right_ref[2])
        o = times_table(jnp.concatenate([re[:, h:], im[:, h:]], 1), right_ref[3])
        br = jnp.concatenate([e[:, :h] + o[:, :h], e[:, :h] - o[:, :h]], 1)
        bi = jnp.concatenate([e[:, h:] + o[:, h:], e[:, h:] - o[:, h:]], 1)
        pr, pi = probe_ref[k, 0].astype(F32), probe_ref[k, 1].astype(F32)
        ot[0] += pr * br + pi * bi
        ot[1] += pr * bi - pi * br
        a, b = patch[0], patch[1]
        return a * br + b * bi, a * bi - b * br

    mode_rows = 2 * ps
    pair = sems(mh)

    def pair_copy(i):
        at = pl.ds(pl.multiple_of(i * mode_rows, mode_rows), mode_rows)
        return remote(sendbuf.at[at], pairbuf.at[at], pair + i, sibling, z)

    def both(i):
        gr, gi = backward((1 - core) * mh + i)
        at = pl.multiple_of(i * mode_rows, mode_rows)
        sendbuf[pl.ds(at, ps)] = gr
        sendbuf[pl.ds(at + ps, ps)] = gi
        pair_copy(i).start()
        gr, gi = backward(core * mh + i)
        pair_copy(i).wait_recv()
        acc[pl.ds(at, ps)] = gr + pairbuf[pl.ds(at, ps)]
        acc[pl.ds(at + ps, ps)] = gi + pairbuf[pl.ds(at + ps, ps)]

    n_streams = streams_of(n_tile, n_batch, mh, mode_rows)
    length = mh * mode_rows // n_streams
    per_stream = mh // n_streams
    stream_sems = 2 * len(bits) + 2 * n_batch + 1
    base_out = core * (mh * mode_rows)

    class Stream:
        def __init__(self, index, order, z_first=False):
            self.index, self.order, self.z_first = index, order, z_first
            self.first = index * length
            self.start, self.size, self.step = self.first, length, 0
            self.slot = 0
            self.sem_rs = stream_base + index * stream_sems
            self.sem_ag = self.sem_rs + len(order)
            self.sem_z = self.sem_ag + len(order)
            self.sem_zg = self.sem_z + n_batch
            self.sem_pair = self.sem_zg + n_batch
            self.trail = []

        def rows(self, at, n):
            return pl.ds(pl.multiple_of(at, n), n)

        def rs_start(self):
            b = self.order[self.step]
            mine = lax.rem(me // b, 2)
            half = self.size // 2
            self.partner = me + b * (1 - 2 * mine)
            self.trail.append((self.start, self.size, self.partner, mine))
            self.copy = remote(
                acc.at[self.rows(self.start + (1 - mine) * half, half)],
                rsbuf.at[self.index, pl.ds(self.slot, half)],
                self.sem_rs + self.step, self.partner, z)
            if self.step or self.z_first:
                self.copy.start()
            self.start = self.start + mine * half
            self.size = half

        def rs_wait(self):
            self.copy.wait()
            at = self.rows(self.start, self.size)
            acc[at] += rsbuf[self.index, self.slot:self.slot + self.size]
            self.slot += self.size
            self.step += 1

        def zf_start(self):
            q = length // n_batch
            self.copies = []
            for d in range(1, n_batch):
                dest = lax.rem(z + d, n_batch)
                c = remote(acc.at[self.rows(self.first + dest * q, q)], zfbuf.at[d],
                           self.sem_z + d, me, dest)
                c.start()
                self.copies.append(c)

        def zf_wait(self):
            for c in self.copies:
                c.wait()
            self.size = length // n_batch
            self.start = self.first + z * self.size
            at = self.rows(self.start, self.size)
            total = acc[at]
            for d in range(1, n_batch):
                total = total + zfbuf[d]
            acc[at] = total

        def settle(self):
            pg_ref[self.rows(base_out + self.start, self.size)] = acc[self.rows(self.start, self.size)]

        def zl_start(self):
            q = length // n_batch
            at = self.rows(base_out + self.first + z * q, q)
            self.copies = []
            for d in range(1, n_batch):
                c = remote(pg_ref.at[at], pg_ref.at[at], self.sem_zg + d, me, lax.rem(z + d, n_batch))
                c.start()
                self.copies.append(c)

        def z_start(self):
            q = self.size // n_batch
            self.q = q
            self.copies = []
            for d in range(1, n_batch):
                dest = lax.rem(z + d, n_batch)
                c = remote(acc.at[self.rows(self.start + dest * q, q)], zbuf.at[self.index, d],
                           self.sem_z + d, me, dest)
                c.start()
                self.copies.append(c)

        def z_wait(self):
            for c in self.copies:
                c.wait()
            total = acc[self.rows(self.start + z * self.q, self.q)]
            for d in range(1, n_batch):
                total = total + zbuf[self.index, d]
            at = self.rows(base_out + self.start + z * self.q, self.q)
            pg_ref[at] = total
            self.copies = []
            for d in range(1, n_batch):
                c = remote(pg_ref.at[at], pg_ref.at[at], self.sem_zg + d, me, lax.rem(z + d, n_batch))
                c.start()
                self.copies.append(c)

        def zg_wait(self):
            for c in self.copies:
                c.wait()

        def ag_start(self):
            self.step -= 1
            start, size, partner, mine = self.trail[self.step]
            at = self.rows(base_out + start + mine * (size // 2), size // 2)
            self.copy = remote(pg_ref.at[at], pg_ref.at[at], self.sem_ag + self.step, partner, z)
            self.copy.start()

        def ag_wait(self):
            self.copy.wait()

        def pair_start(self):
            at = self.rows(base_out + self.first, length)
            self.copy = remote(pg_ref.at[at], pg_ref.at[at], self.sem_pair, sibling, z)
            self.copy.start()

    stream_base = sems(n_streams * stream_sems)

    def summed(i, carry):
        for j in range(per_stream):
            both(i * per_stream + j)
        bit = bits[0] + lax.rem(i, 2) * (bits[-1] - bits[0])
        mine = lax.rem(me // bit, 2)
        half = length // 2
        at = pl.multiple_of(i * length + (1 - mine) * half, half)
        remote(acc.at[pl.ds(at, half)], rsbuf.at[i, pl.ds(0, half)],
               stream_base + i * stream_sems, me + bit * (1 - 2 * mine), z).start()
        return carry

    for j in range(per_stream):
        both(j)
    around_z = Stream(0, bits, True)
    around_z.zf_start()
    lax.fori_loop(1, n_streams, summed, 0)
    streams = [Stream(i, bits if i % 2 == 0 else bits[::-1]) for i in range(1, n_streams)]
    for s in streams:
        s.rs_start()

    osem = sems(4 * n_batch)
    hops = n_batch - 1

    def sem_of(way, stage, part):
        return osem + stage + n_batch * (2 * part + (1 if way < 0 else 0))

    def passing(way, stage, part):
        origin = z - way * stage
        sends = jnp.logical_and(
            jnp.logical_and(origin >= 0, origin < n_batch),
            jnp.logical_and(z + way >= 0, z + way < n_batch))
        at = jnp.clip(origin, 0, n_batch - 1)
        src = ot.at[part] if stage == 0 else objbuf.at[at, part]
        to = jnp.clip(z + way, 0, n_batch - 1)
        return sends, remote(src, objbuf.at[at, part], sem_of(way, stage, part), me, to)

    def arrival(way, stage, part):
        origin = z - way * (1 + stage)
        comes = jnp.logical_and(origin >= 0, origin < n_batch)
        at = jnp.clip(origin, 0, n_batch - 1)
        return comes, at, remote(ot.at[part], objbuf.at[at, part], sem_of(way, stage, part),
                                 me, jnp.clip(z + way, 0, n_batch - 1))

    def start_passing(stage, part):
        for way in (1, -1):
            sends, c = passing(way, stage, part)

            @pl.when(sends)
            def _():
                c.start()

    def place(offs, term):
        put_r = onehot(lax.broadcasted_iota(jnp.int32, (te, ps), 0)
                       == lax.broadcasted_iota(jnp.int32, (te, ps), 1) + offs[0:1, 0:1])
        put_c = onehot(lax.broadcasted_iota(jnp.int32, (ps, te), 1)
                       == lax.broadcasted_iota(jnp.int32, (ps, te), 0) + offs[1:2, 0:1])
        return onehot_times(put_r, times_onehot(term, put_c))

    right_sem, down_sem = sems(2), sems(2)
    rightward = [remote(gext.at[part, :, ts:], xbuf.at[part], right_sem + part, me + 1, z)
                 for part in range(2)]
    downward = [remote(gext.at[part, ts:, :ts], ybuf.at[part], down_sem + part, me + TILE_COLS, z)
                for part in range(2)]

    def arrived(stage, part):
        for way in (1, -1):
            comes, at, c = arrival(way, stage, part)

            @pl.when(comes)
            def _():
                c.wait_recv()
        if stage + 1 < hops:
            start_passing(stage + 1, part)
        if part == 0 and stage == max(hops - 2, 0):
            start_passing(0, 1)
        for way in (1, -1):
            comes, at, c = arrival(way, stage, part)
            slot = stage + 1 if way > 0 else n_batch - 1 - stage

            @pl.when(comes)
            def _():
                gext[part] += place(offbuf.at[slot], objbuf[at, part])

        if stage + 1 == hops:
            @pl.when(has_right)
            def _():
                rightward[part].start()

    def margin(part):
        @pl.when(has_left)
        def _():
            rightward[part].wait_recv()
            gext[part, :, :ps] += xbuf[part]

        @pl.when(has_down)
        def _():
            downward[part].start()

    start_passing(0, 0)
    for part in range(2):
        gext[part] = place(off_ref, ot[part])
    for c in offs_out:
        c.wait()

    todo = [functools.partial(arrived, stage, part) for part in range(2) for stage in range(hops)]

    def serve():
        if todo:
            todo.pop(0)()

    for step in range(len(bits)):
        serve()
        if step == 0:
            around_z.zf_wait()
        else:
            around_z.rs_wait()
        around_z.rs_start()
        for s in streams:
            s.rs_wait()
            if step + 1 < len(bits):
                s.rs_start()
            else:
                s.z_start()
    while len(todo) > hops:
        serve()
    around_z.rs_wait()
    around_z.settle()
    around_z.ag_start()
    for s in streams:
        s.z_wait()
    while len(todo) > 2:
        serve()
    for step in range(len(bits) - 1):
        around_z.ag_wait()
        around_z.ag_start()
    margin(0)
    for s in streams:
        s.zg_wait()
        s.ag_start()
    while todo:
        serve()
    around_z.ag_wait()
    around_z.zl_start()
    for step in range(len(bits)):
        for s in streams:
            s.ag_wait()
            if step + 1 < len(bits):
                s.ag_start()
            else:
                s.pair_start()
        if step == 0:
            margin(1)
    around_z.zg_wait()
    around_z.pair_start()

    outs = []

    def write_out(src, dst):
        c = pltpu.make_async_copy(src, dst, out_sem.at[len(outs)])
        c.start()
        outs.append(c)

    def write_stream(s):
        s.copy.wait()
        for side in range(2):
            at = pl.ds(side * mh * mode_rows + s.first, length)
            write_out(pg_ref.at[at], pg_hbm.at[at])

    for s in streams:
        write_stream(s)
    for part in range(2):
        og_ref[part] = gext[part, :ts, :ts]

        @pl.when(has_up)
        def _():
            downward[part].wait_recv()
            og_ref[part, :ps, :] += ybuf[part]

        write_out(og_ref.at[part], og_hbm.at[part])
    write_stream(around_z)

    for part in range(2):
        @pl.when(has_right)
        def _():
            rightward[part].wait_send()

        @pl.when(has_down)
        def _():
            downward[part].wait_send()

    for part in range(2):
        for stage in range(hops):
            for way in (1, -1):
                sends, c = passing(way, stage, part)

                @pl.when(sends)
                def _():
                    c.wait_send()

    def sent(i, carry):
        pair_copy(i).wait_send()
        return carry

    lax.fori_loop(0, mh, sent, 0)
    for c in outs:
        c.wait()


def streams_of(n_tile, n_batch, mh, mode_rows):
    return mh if mode_rows // (n_tile // 2) // n_batch >= 8 else 2


def n_sems(n_tile, n_batch, mh, n_streams):
    n_bits = n_tile.bit_length() - 2
    return 7 + mh + n_streams * (2 * n_bits + 2 * n_batch + 1) + 5 * n_batch + 4


def shards(n_tile, n_batch, object_tiles, probe, offsets, amplitude):
    modes, _, ps, _ = probe.shape
    ts = object_tiles.shape[-1]
    te = ts + ps
    rights, lefts = dft_tables(ps)
    n_streams = streams_of(n_tile, n_batch, modes // 2, 2 * ps)
    n = n_sems(n_tile, n_batch, modes // 2, n_streams)
    half = modes // 2 * 2 * ps
    length = half // n_streams
    q = length // (n_tile // 2) // n_batch
    vmem = pl.BlockSpec(memory_space=pltpu.VMEM)
    smem = pl.BlockSpec(memory_space=pltpu.SMEM)
    anywhere = pl.BlockSpec(memory_space=pl.ANY)
    og, pg = pl.pallas_call(
        functools.partial(kernel, n_tile, n_batch),
        out_shape=(jax.ShapeDtypeStruct((2, ts, ts), F32),
                   jax.ShapeDtypeStruct((modes * 2 * ps, ps), F32)),
        in_specs=[vmem, smem, anywhere, anywhere, anywhere, anywhere],
        out_specs=(anywhere, anywhere),
        scratch_shapes=[
            pltpu.VMEM((ps, ps), F32),
            pltpu.VMEM(probe.shape, probe.dtype),
            pltpu.VMEM(rights.shape, BF16),
            pltpu.VMEM(lefts.shape, BF16),
            pltpu.VMEM((8, 128), jnp.int32),
            pltpu.VMEM((2, ts, ts), F32),
            pltpu.VMEM((modes * 2 * ps, ps), F32),
            pltpu.VMEM((2, te, te), F32),
            pltpu.VMEM((2, ps, ps), F32),
            pltpu.VMEM((modes, 2, ps, ps), F32),
            pltpu.VMEM((ps, ps), F32),
            pltpu.VMEM((2, ps, ps), F32),
            pltpu.VMEM((2, te, te), F32),
            pltpu.VMEM((half, ps), F32),
            pltpu.VMEM((half, ps), F32),
            pltpu.VMEM((half, ps), F32),
            pltpu.VMEM((n_streams, length, ps), F32),
            pltpu.VMEM((n_streams, n_batch, q, ps), F32),
            pltpu.VMEM((n_batch, length // n_batch, ps), F32),
            pltpu.VMEM((n_batch, 2, ps, ps), F32),
            pltpu.VMEM((n_batch, 8, 128), jnp.int32),
            pltpu.VMEM((2, te, ps), F32),
            pltpu.VMEM((2, ps, ts), F32),
            pltpu.SemaphoreType.DMA((n,)),
            pltpu.SemaphoreType.DMA((n,)),
            pltpu.SemaphoreType.DMA((4,)),
            pltpu.SemaphoreType.DMA((2 * n_streams + 2,)),
        ],
        compiler_params=pltpu.CompilerParams(
            collective_id=0, has_side_effects=True, vmem_limit_bytes=56 * 1024 * 1024),
        cost_estimate=pl.CostEstimate(flops=13_000_000_000, bytes_accessed=20_000_000, transcendentals=0),
        name="ptycho",
    )(object_tiles[0], offsets, amplitude[0, 0], probe, rights, lefts)
    positions = n_tile * n_batch * offsets.shape[1]
    return og[None], pg.reshape(modes, 2, ps, ps) * (1.0 / math.sqrt(positions))


def solution(mesh):
    placed = (
        P("tile", None, None, None),
        P(),
        P("tile", "batch", None),
        P("tile", "batch", None, None),
    )
    return jax.shard_map(
        functools.partial(shards, mesh.shape["tile"], mesh.shape["batch"]),
        mesh=mesh,
        in_specs=placed,
        out_specs=(P("tile", None, None, None), P()),
        check_vma=False,
    )
```

```python
import functools
import math

import jax
import jax.numpy as jnp
import ml_dtypes
import numpy as np
from jax import lax
from jax.experimental import pallas as pl
from jax.experimental.pallas import tpu as pltpu
from jax.sharding import PartitionSpec as P

TILE_COLS = 4
MESH = pl.DeviceIdType.MESH
F32 = jnp.float32
BF16 = jnp.bfloat16


def split_table(table, axis):
    high = table.astype(np.float32).astype(ml_dtypes.bfloat16)
    low = (table - high.astype(np.float64)).astype(np.float32).astype(ml_dtypes.bfloat16)
    return np.concatenate([high, high, low], axis=axis)


def dft_tables(pattern):
    h = pattern // 2
    n, k = np.arange(h)[:, None], np.arange(h)[None, :]
    even = np.exp(-2j * np.pi * ((2 * n * k) % pattern) / pattern) / math.sqrt(pattern)
    odd = np.exp(-2j * np.pi * ((n * (2 * k + 1)) % pattern) / pattern) / math.sqrt(pattern)

    def right(m):
        return split_table(np.block([[m.real, m.imag], [-m.imag, m.real]]), 0)

    def left(m):
        return split_table(np.block([[m.real, -m.imag], [m.imag, m.real]]), 1)

    rights = np.stack([right(even), right(odd), right(even.conj().T), right(odd.conj().T)])
    lefts = np.stack([left(even.T), left(odd.T), left(even.conj()), left(odd.conj())])
    return rights, lefts


def split(x):
    high = x.astype(BF16)
    return high, (x - high.astype(F32)).astype(BF16)


def times_table(x, table):
    high, low = split(x)
    return jnp.dot(jnp.concatenate([high, low, high], 1), table, preferred_element_type=F32)


def table_times(table, x):
    high, low = split(x)
    return jnp.dot(table, jnp.concatenate([high, low, high], 0), preferred_element_type=F32)


def times_onehot(x, onehot):
    high, low = split(x)
    return jnp.dot(high, onehot, preferred_element_type=F32) + jnp.dot(
        low, onehot, preferred_element_type=F32
    )


def onehot_times(onehot, x):
    high, low = split(x)
    return jnp.dot(onehot, high, preferred_element_type=F32) + jnp.dot(
        onehot, low, preferred_element_type=F32
    )


def onehot(hit):
    return jnp.where(hit, 1.0, 0.0).astype(F32).astype(BF16)


def kernel(n_tile, n_batch, tile_ref, offsets_ref, amp_hbm, probe_hbm, right_hbm, left_hbm,
           og_hbm, pg_hbm, amp_ref, probe_ref, right_ref, left_ref, off_ref, og_ref, pg_ref, ext, patch, far, fac, ot, gext, acc, sendbuf, pairbuf, rsbuf, zbuf, zfbuf,
           objbuf, offbuf, xbuf, ybuf, send_sem, recv_sem, load_sem,
           out_sem):
    me = lax.axis_index("tile")
    z = lax.axis_index("batch")
    ts = tile_ref.shape[-1]
    modes, _, ps, _ = probe_ref.shape
    h = ps // 2
    mh = modes // 2
    bits = []
    b = 2
    while b < n_tile:
        bits.append(b)
        b *= 2
    core = lax.rem(me, 2)
    sibling = me + 1 - 2 * core
    col = lax.rem(me, TILE_COLS)
    has_left = col > 0
    has_right = col < TILE_COLS - 1
    has_up = me >= TILE_COLS
    has_down = me < n_tile - TILE_COLS
    count = [0]

    def sems(n=1):
        first = count[0]
        count[0] += n
        return first

    def remote(src, dst, sem, tile, batch):
        return pltpu.make_async_remote_copy(
            src_ref=src, dst_ref=dst, send_sem=send_sem.at[sem], recv_sem=recv_sem.at[sem],
            device_id=(tile, batch), device_id_type=MESH)

    loads = [pltpu.make_async_copy(src, dst, load_sem.at[i]) for i, (src, dst) in enumerate(
        ((amp_hbm, amp_ref), (probe_hbm, probe_ref), (right_hbm, right_ref), (left_hbm, left_ref)))]
    for c in loads:
        c.start()
    off_ref[...] = jnp.where(lax.broadcasted_iota(jnp.int32, off_ref.shape, 0) == 0,
                             offsets_ref[0, 0, 0], offsets_ref[0, 0, 1])

    barrier = pltpu.get_barrier_semaphore()

    def greet(tile, batch):
        pl.semaphore_signal(barrier, inc=1, device_id=(tile, batch), device_id_type=MESH)

    greet(sibling, z)
    for b in bits:
        greet(me + b * (1 - 2 * lax.rem(me // b, 2)), z)
    for d in range(1, n_batch):
        greet(me, lax.rem(z + d, n_batch))
    for there, step in ((has_left, -1), (has_right, 1), (has_up, -TILE_COLS), (has_down, TILE_COLS)):
        @pl.when(there)
        def _():
            greet(me + step, z)
    around = sum(jnp.where(t, 1, 0) for t in (has_left, has_right, has_up, has_down))
    pl.semaphore_wait(barrier, 1 + len(bits) + n_batch - 1 + around)

    fsem = sems(n_batch)
    offs_out = [remote(off_ref, offbuf.at[d], fsem + d, me, lax.rem(z + d, n_batch))
                for d in range(1, n_batch)]
    for c in offs_out:
        c.start()

    own = lax.rem(z, 2)
    twin = z + 1 - 2 * own
    pieces = (slice(0, ps), slice(ps, ts))
    up = [remote(tile_ref.at[own, :ps, c], ext.at[own, ts:, c], sems(), me - TILE_COLS, z)
          for c in pieces]
    share = [remote(ext.at[own, ts:, c], ext.at[own, ts:, c], sems(), me, twin) for c in pieces]
    leftward = remote(tile_ref.at[:, :, :ps], ext.at[:, :ts, ts:], sems(), me - 1, z)
    corner = [remote(ext.at[part, ts:, :ps], ext.at[part, ts:, ts:], sems(), me - 1, z)
              for part in (own, 1 - own)]

    @pl.when(has_up)
    def _():
        up[0].start()
        up[1].start()

    @pl.when(has_left)
    def _():
        leftward.start()

    ext[:, :ts, :ts] = tile_ref[...]

    @pl.when(jnp.logical_not(has_right))
    def _():
        ext[:, :, ts:] = jnp.zeros((2, ts + ps, ps), F32)

    @pl.when(jnp.logical_not(has_down))
    def _():
        ext[:, ts:, :ts] = jnp.zeros((2, ps, ts), F32)

    @pl.when(jnp.logical_and(jnp.logical_not(has_down), has_right))
    def _():
        ext[:, ts:, ts:] = jnp.zeros((2, ps, ps), F32)

    loads[0].wait()
    rows = lax.broadcasted_iota(jnp.int32, (ps, ps), 0)
    cols = lax.broadcasted_iota(jnp.int32, (ps, ps), 1)
    by_row = onehot(cols == jnp.where(rows < h, 2 * rows, 2 * (rows - h) + 1))
    by_col = onehot(rows == jnp.where(cols < h, 2 * cols, 2 * (cols - h) + 1))
    fac[...] = times_onehot(onehot_times(by_row, amp_ref[...]), by_col)

    @pl.when(has_down)
    def _():
        up[0].wait_recv()
        share[0].start()

    @pl.when(jnp.logical_and(has_down, has_left))
    def _():
        corner[0].start()

    @pl.when(has_down)
    def _():
        up[1].wait_recv()
        share[1].start()
        share[0].wait_recv()

    @pl.when(jnp.logical_and(has_down, has_left))
    def _():
        corner[1].start()

    @pl.when(has_down)
    def _():
        share[1].wait_recv()

    @pl.when(has_right)
    def _():
        leftward.wait_recv()

    @pl.when(jnp.logical_and(has_down, has_right))
    def _():
        corner[0].wait_recv()
        corner[1].wait_recv()

    r_at = off_ref[0:1, 0:1]
    c_at = off_ref[1:2, 0:1]
    te = ts + ps
    pick_r = onehot(lax.broadcasted_iota(jnp.int32, (ps, te), 1)
                    == lax.broadcasted_iota(jnp.int32, (ps, te), 0) + r_at)
    pick_c = onehot(lax.broadcasted_iota(jnp.int32, (te, ps), 0)
                    == lax.broadcasted_iota(jnp.int32, (te, ps), 1) + c_at)
    for part in range(2):
        patch[part] = times_onehot(onehot_times(pick_r, ext[part]), pick_c)

    @pl.when(has_up)
    def _():
        up[0].wait_send()
        up[1].wait_send()

    @pl.when(has_left)
    def _():
        leftward.wait_send()

    @pl.when(jnp.logical_and(has_down, has_left))
    def _():
        corner[0].wait_send()
        corner[1].wait_send()

    @pl.when(has_down)
    def _():
        share[0].wait_send()
        share[1].wait_send()

    for c in loads[1:]:
        c.wait()

    def forward(k, intensity):
        i0, i1 = intensity
        pr, pi = probe_ref[k, 0].astype(F32), probe_ref[k, 1].astype(F32)
        a, b = patch[0], patch[1]
        xr, xi = pr * a - pi * b, pr * b + pi * a
        plus = jnp.concatenate([xr[:, :h] + xr[:, h:], xi[:, :h] + xi[:, h:]], 1)
        minus = jnp.concatenate([xr[:, :h] - xr[:, h:], xi[:, :h] - xi[:, h:]], 1)
        e = times_table(plus, right_ref[0])
        o = times_table(minus, right_ref[1])
        re = jnp.concatenate([e[:, :h], o[:, :h]], 1)
        im = jnp.concatenate([e[:, h:], o[:, h:]], 1)
        g = table_times(left_ref[0], jnp.concatenate([re[:h] + re[h:], im[:h] + im[h:]], 0))
        f = table_times(left_ref[1], jnp.concatenate([re[:h] - re[h:], im[:h] - im[h:]], 0))
        far[k, 0] = g
        far[k, 1] = f
        return (i0 + g[:h] * g[:h] + g[h:] * g[h:], i1 + f[:h] * f[:h] + f[h:] * f[h:])

    zero = jnp.zeros((h, ps), F32)
    i0, i1 = lax.fori_loop(
        0, modes // 2, lambda i, c: forward(2 * i + 1, forward(2 * i, c)), (zero, zero))
    fac[:h] = 1.0 - fac[:h] / jnp.sqrt(i0 + 0.01)
    fac[h:] = 1.0 - fac[h:] / jnp.sqrt(i1 + 0.01)
    ot[...] = jnp.zeros_like(ot)

    def backward(k):
        f0, f1 = fac[:h], fac[h:]
        g = far[k, 0] * jnp.concatenate([f0, f0], 0)
        f = far[k, 1] * jnp.concatenate([f1, f1], 0)
        p = table_times(left_ref[2], g)
        q = table_times(left_ref[3], f)
        top, low = p + q, p - q
        re = jnp.concatenate([top[:h], low[:h]], 0)
        im = jnp.concatenate([top[h:], low[h:]], 0)
        e = times_table(jnp.concatenate([re[:, :h], im[:, :h]], 1), right_ref[2])
        o = times_table(jnp.concatenate([re[:, h:], im[:, h:]], 1), right_ref[3])
        br = jnp.concatenate([e[:, :h] + o[:, :h], e[:, :h] - o[:, :h]], 1)
        bi = jnp.concatenate([e[:, h:] + o[:, h:], e[:, h:] - o[:, h:]], 1)
        pr, pi = probe_ref[k, 0].astype(F32), probe_ref[k, 1].astype(F32)
        ot[0] += pr * br + pi * bi
        ot[1] += pr * bi - pi * br
        a, b = patch[0], patch[1]
        return a * br + b * bi, a * bi - b * br

    mode_rows = 2 * ps
    pair = sems(mh)

    def pair_copy(i):
        at = pl.ds(pl.multiple_of(i * mode_rows, mode_rows), mode_rows)
        return remote(sendbuf.at[at], pairbuf.at[at], pair + i, sibling, z)

    def both(i):
        gr, gi = backward((1 - core) * mh + i)
        at = pl.multiple_of(i * mode_rows, mode_rows)
        sendbuf[pl.ds(at, ps)] = gr
        sendbuf[pl.ds(at + ps, ps)] = gi
        pair_copy(i).start()
        gr, gi = backward(core * mh + i)
        pair_copy(i).wait_recv()
        acc[pl.ds(at, ps)] = gr + pairbuf[pl.ds(at, ps)]
        acc[pl.ds(at + ps, ps)] = gi + pairbuf[pl.ds(at + ps, ps)]

    n_streams = streams_of(n_tile, n_batch, mh, mode_rows)
    length = mh * mode_rows // n_streams
    per_stream = mh // n_streams
    stream_sems = 2 * len(bits) + 2 * n_batch + 1
    base_out = core * (mh * mode_rows)

    class Stream:
        def __init__(self, index, order, z_first=False):
            self.index, self.order, self.z_first = index, order, z_first
            self.first = index * length
            self.start, self.size, self.step = self.first, length, 0
            self.slot = 0
            self.sem_rs = stream_base + index * stream_sems
            self.sem_ag = self.sem_rs + len(order)
            self.sem_z = self.sem_ag + len(order)
            self.sem_zg = self.sem_z + n_batch
            self.sem_pair = self.sem_zg + n_batch
            self.trail = []

        def rows(self, at, n):
            return pl.ds(pl.multiple_of(at, n), n)

        def rs_start(self):
            b = self.order[self.step]
            mine = lax.rem(me // b, 2)
            half = self.size // 2
            self.partner = me + b * (1 - 2 * mine)
            self.trail.append((self.start, self.size, self.partner, mine))
            self.copy = remote(
                acc.at[self.rows(self.start + (1 - mine) * half, half)],
                rsbuf.at[self.index, pl.ds(self.slot, half)],
                self.sem_rs + self.step, self.partner, z)
            if self.step or self.z_first:
                self.copy.start()
            self.start = self.start + mine * half
            self.size = half

        def rs_wait(self):
            self.copy.wait()
            at = self.rows(self.start, self.size)
            acc[at] += rsbuf[self.index, self.slot:self.slot + self.size]
            self.slot += self.size
            self.step += 1

        def zf_start(self):
            q = length // n_batch
            self.copies = []
            for d in range(1, n_batch):
                dest = lax.rem(z + d, n_batch)
                c = remote(acc.at[self.rows(self.first + dest * q, q)], zfbuf.at[d],
                           self.sem_z + d, me, dest)
                c.start()
                self.copies.append(c)

        def zf_wait(self):
            for c in self.copies:
                c.wait()
            self.size = length // n_batch
            self.start = self.first + z * self.size
            at = self.rows(self.start, self.size)
            total = acc[at]
            for d in range(1, n_batch):
                total = total + zfbuf[d]
            acc[at] = total

        def settle(self):
            pg_ref[self.rows(base_out + self.start, self.size)] = acc[self.rows(self.start, self.size)]

        def zl_start(self):
            q = length // n_batch
            at = self.rows(base_out + self.first + z * q, q)
            self.copies = []
            for d in range(1, n_batch):
                c = remote(pg_ref.at[at], pg_ref.at[at], self.sem_zg + d, me, lax.rem(z + d, n_batch))
                c.start()
                self.copies.append(c)

        def z_start(self):
            q = self.size // n_batch
            self.q = q
            self.copies = []
            for d in range(1, n_batch):
                dest = lax.rem(z + d, n_batch)
                c = remote(acc.at[self.rows(self.start + dest * q, q)], zbuf.at[self.index, d],
                           self.sem_z + d, me, dest)
                c.start()
                self.copies.append(c)

        def z_wait(self):
            for c in self.copies:
                c.wait()
            total = acc[self.rows(self.start + z * self.q, self.q)]
            for d in range(1, n_batch):
                total = total + zbuf[self.index, d]
            at = self.rows(base_out + self.start + z * self.q, self.q)
            pg_ref[at] = total
            self.copies = []
            for d in range(1, n_batch):
                c = remote(pg_ref.at[at], pg_ref.at[at], self.sem_zg + d, me, lax.rem(z + d, n_batch))
                c.start()
                self.copies.append(c)

        def zg_wait(self):
            for c in self.copies:
                c.wait()

        def ag_start(self):
            self.step -= 1
            start, size, partner, mine = self.trail[self.step]
            at = self.rows(base_out + start + mine * (size // 2), size // 2)
            self.copy = remote(pg_ref.at[at], pg_ref.at[at], self.sem_ag + self.step, partner, z)
            self.copy.start()

        def ag_wait(self):
            self.copy.wait()

        def pair_start(self):
            at = self.rows(base_out + self.first, length)
            self.copy = remote(pg_ref.at[at], pg_ref.at[at], self.sem_pair, sibling, z)
            self.copy.start()

    stream_base = sems(n_streams * stream_sems)

    def summed(i, carry):
        for j in range(per_stream):
            both(i * per_stream + j)
        bit = bits[0] + lax.rem(i, 2) * (bits[-1] - bits[0])
        mine = lax.rem(me // bit, 2)
        half = length // 2
        at = pl.multiple_of(i * length + (1 - mine) * half, half)
        remote(acc.at[pl.ds(at, half)], rsbuf.at[i, pl.ds(0, half)],
               stream_base + i * stream_sems, me + bit * (1 - 2 * mine), z).start()
        return carry

    for j in range(per_stream):
        both(j)
    around_z = Stream(0, bits, True)
    around_z.zf_start()
    lax.fori_loop(1, n_streams, summed, 0)
    streams = [Stream(i, bits if i % 2 == 0 else bits[::-1]) for i in range(1, n_streams)]
    for s in streams:
        s.rs_start()

    osem = sems(4 * n_batch)
    hops = n_batch - 1

    def sem_of(way, stage, part):
        return osem + stage + n_batch * (2 * part + (1 if way < 0 else 0))

    def passing(way, stage, part):
        origin = z - way * stage
        sends = jnp.logical_and(
            jnp.logical_and(origin >= 0, origin < n_batch),
            jnp.logical_and(z + way >= 0, z + way < n_batch))
        at = jnp.clip(origin, 0, n_batch - 1)
        src = ot.at[part] if stage == 0 else objbuf.at[at, part]
        to = jnp.clip(z + way, 0, n_batch - 1)
        return sends, remote(src, objbuf.at[at, part], sem_of(way, stage, part), me, to)

    def arrival(way, stage, part):
        origin = z - way * (1 + stage)
        comes = jnp.logical_and(origin >= 0, origin < n_batch)
        at = jnp.clip(origin, 0, n_batch - 1)
        return comes, at, remote(ot.at[part], objbuf.at[at, part], sem_of(way, stage, part),
                                 me, jnp.clip(z + way, 0, n_batch - 1))

    def start_passing(stage, part):
        for way in (1, -1):
            sends, c = passing(way, stage, part)

            @pl.when(sends)
            def _():
                c.start()

    def place(offs, term):
        put_r = onehot(lax.broadcasted_iota(jnp.int32, (te, ps), 0)
                       == lax.broadcasted_iota(jnp.int32, (te, ps), 1) + offs[0:1, 0:1])
        put_c = onehot(lax.broadcasted_iota(jnp.int32, (ps, te), 1)
                       == lax.broadcasted_iota(jnp.int32, (ps, te), 0) + offs[1:2, 0:1])
        return onehot_times(put_r, times_onehot(term, put_c))

    right_sem, down_sem = sems(2), sems(2)
    rightward = [remote(gext.at[part, :, ts:], xbuf.at[part], right_sem + part, me + 1, z)
                 for part in range(2)]
    downward = [remote(gext.at[part, ts:, :ts], ybuf.at[part], down_sem + part, me + TILE_COLS, z)
                for part in range(2)]

    def arrived(stage, part):
        for way in (1, -1):
            comes, at, c = arrival(way, stage, part)

            @pl.when(comes)
            def _():
                c.wait_recv()
        if stage + 1 < hops:
            start_passing(stage + 1, part)
        if part == 0 and stage == max(hops - 2, 0):
            start_passing(0, 1)
        for way in (1, -1):
            comes, at, c = arrival(way, stage, part)
            slot = stage + 1 if way > 0 else n_batch - 1 - stage

            @pl.when(comes)
            def _():
                gext[part] += place(offbuf.at[slot], objbuf[at, part])

        if stage + 1 == hops:
            @pl.when(has_right)
            def _():
                rightward[part].start()

    def margin(part):
        @pl.when(has_left)
        def _():
            rightward[part].wait_recv()
            gext[part, :, :ps] += xbuf[part]

        @pl.when(has_down)
        def _():
            downward[part].start()

    start_passing(0, 0)
    for part in range(2):
        gext[part] = place(off_ref, ot[part])
    for c in offs_out:
        c.wait()

    todo = [functools.partial(arrived, stage, part) for part in range(2) for stage in range(hops)]

    def serve():
        if todo:
            todo.pop(0)()

    for step in range(len(bits)):
        serve()
        if step == 0:
            around_z.zf_wait()
        else:
            around_z.rs_wait()
        around_z.rs_start()
        for s in streams:
            s.rs_wait()
            if step + 1 < len(bits):
                s.rs_start()
            else:
                s.z_start()
    while len(todo) > hops:
        serve()
    around_z.rs_wait()
    around_z.settle()
    around_z.ag_start()
    for s in streams:
        s.z_wait()
    while len(todo) > 2:
        serve()
    for step in range(len(bits) - 1):
        around_z.ag_wait()
        around_z.ag_start()
    margin(0)
    for s in streams:
        s.zg_wait()
        s.ag_start()
    while todo:
        serve()
    around_z.ag_wait()
    around_z.zl_start()
    for step in range(len(bits)):
        for s in streams:
            s.ag_wait()
            if step + 1 < len(bits):
                s.ag_start()
            else:
                s.pair_start()
        if step == 0:
            margin(1)
    around_z.zg_wait()
    around_z.pair_start()

    outs = []

    def write_out(src, dst):
        c = pltpu.make_async_copy(src, dst, out_sem.at[len(outs)])
        c.start()
        outs.append(c)

    def write_stream(s):
        s.copy.wait()
        for side in range(2):
            at = pl.ds(side * mh * mode_rows + s.first, length)
            write_out(pg_ref.at[at], pg_hbm.at[at])

    for s in streams:
        write_stream(s)
    for part in range(2):
        og_ref[part] = gext[part, :ts, :ts]

        @pl.when(has_up)
        def _():
            downward[part].wait_recv()
            og_ref[part, :ps, :] += ybuf[part]

        write_out(og_ref.at[part], og_hbm.at[part])
    write_stream(around_z)

    for part in range(2):
        @pl.when(has_right)
        def _():
            rightward[part].wait_send()

        @pl.when(has_down)
        def _():
            downward[part].wait_send()

    for part in range(2):
        for stage in range(hops):
            for way in (1, -1):
                sends, c = passing(way, stage, part)

                @pl.when(sends)
                def _():
                    c.wait_send()

    def sent(i, carry):
        pair_copy(i).wait_send()
        return carry

    lax.fori_loop(0, mh, sent, 0)
    for c in outs:
        c.wait()


def streams_of(n_tile, n_batch, mh, mode_rows):
    return mh if mode_rows // (n_tile // 2) // n_batch >= 8 else 2


def n_sems(n_tile, n_batch, mh, n_streams):
    n_bits = n_tile.bit_length() - 2
    return 7 + mh + n_streams * (2 * n_bits + 2 * n_batch + 1) + 5 * n_batch + 4


def finish(scale, og_ref, pg_ref, og_out, pg_out):
    og_out[...] = og_ref[...]
    pg_out[...] = pg_ref[...] * scale


def shards(n_tile, n_batch, object_tiles, probe, offsets, amplitude):
    modes, _, ps, _ = probe.shape
    ts = object_tiles.shape[-1]
    te = ts + ps
    rights, lefts = dft_tables(ps)
    n_streams = streams_of(n_tile, n_batch, modes // 2, 2 * ps)
    n = n_sems(n_tile, n_batch, modes // 2, n_streams)
    half = modes // 2 * 2 * ps
    length = half // n_streams
    q = length // (n_tile // 2) // n_batch
    vmem = pl.BlockSpec(memory_space=pltpu.VMEM)
    smem = pl.BlockSpec(memory_space=pltpu.SMEM)
    anywhere = pl.BlockSpec(memory_space=pl.ANY)
    og, pg = pl.pallas_call(
        functools.partial(kernel, n_tile, n_batch),
        out_shape=(jax.ShapeDtypeStruct((2, ts, ts), F32),
                   jax.ShapeDtypeStruct((modes * 2 * ps, ps), F32)),
        in_specs=[vmem, smem, anywhere, anywhere, anywhere, anywhere],
        out_specs=(anywhere, anywhere),
        scratch_shapes=[
            pltpu.VMEM((ps, ps), F32),
            pltpu.VMEM(probe.shape, probe.dtype),
            pltpu.VMEM(rights.shape, BF16),
            pltpu.VMEM(lefts.shape, BF16),
            pltpu.VMEM((8, 128), jnp.int32),
            pltpu.VMEM((2, ts, ts), F32),
            pltpu.VMEM((modes * 2 * ps, ps), F32),
            pltpu.VMEM((2, te, te), F32),
            pltpu.VMEM((2, ps, ps), F32),
            pltpu.VMEM((modes, 2, ps, ps), F32),
            pltpu.VMEM((ps, ps), F32),
            pltpu.VMEM((2, ps, ps), F32),
            pltpu.VMEM((2, te, te), F32),
            pltpu.VMEM((half, ps), F32),
            pltpu.VMEM((half, ps), F32),
            pltpu.VMEM((half, ps), F32),
            pltpu.VMEM((n_streams, length, ps), F32),
            pltpu.VMEM((n_streams, n_batch, q, ps), F32),
            pltpu.VMEM((n_batch, length // n_batch, ps), F32),
            pltpu.VMEM((n_batch, 2, ps, ps), F32),
            pltpu.VMEM((n_batch, 8, 128), jnp.int32),
            pltpu.VMEM((2, te, ps), F32),
            pltpu.VMEM((2, ps, ts), F32),
            pltpu.SemaphoreType.DMA((n,)),
            pltpu.SemaphoreType.DMA((n,)),
            pltpu.SemaphoreType.DMA((4,)),
            pltpu.SemaphoreType.DMA((2 * n_streams + 2,)),
        ],
        compiler_params=pltpu.CompilerParams(
            collective_id=0, has_side_effects=True, vmem_limit_bytes=56 * 1024 * 1024),
        cost_estimate=pl.CostEstimate(flops=13_000_000_000, bytes_accessed=20_000_000, transcendentals=0),
        name="ptycho",
    )(object_tiles[0], offsets, amplitude[0, 0], probe, rights, lefts)
    positions = n_tile * n_batch * offsets.shape[1]
    probe_spec = pl.BlockSpec((modes * 2 * ps // 8, ps), lambda i: (i, 0))
    object_spec = pl.BlockSpec((2, ts // 8, ts), lambda i: (0, i, 0))
    og, pg = pl.pallas_call(
        functools.partial(finish, 1.0 / math.sqrt(positions)),
        out_shape=(jax.ShapeDtypeStruct(og.shape, F32), jax.ShapeDtypeStruct(pg.shape, F32)),
        grid=(8,),
        in_specs=[object_spec, probe_spec],
        out_specs=(object_spec, probe_spec),
        name="finish",
    )(og, pg)
    return og[None], pg.reshape(modes, 2, ps, ps)


def solution(mesh):
    placed = (
        P("tile", None, None, None),
        P(),
        P("tile", "batch", None),
        P("tile", "batch", None, None),
    )
    return jax.shard_map(
        functools.partial(shards, mesh.shape["tile"], mesh.shape["batch"]),
        mesh=mesh,
        in_specs=placed,
        out_specs=(P("tile", None, None, None), P()),
        check_vma=False,
    )
```
